128 devices in a mesh: pin: 32 (over z, x, core), board: 4 (over y).
Axes of the slice: x: 4, y: 4, z: 4, core: 2. Of those that a mesh axis runs over, the one named last changes fastest.
Arguments:
- features: bfloat16 [65536, 2048], P(('pin', 'board')), may hold values from -6 to 6
- w_message: bfloat16 [2048, 1024], replicated, may hold values from -0.125 to 0.125
- w_update: bfloat16 [1024, 1024], replicated, may hold values from -0.375 to 0.375
- cotangent: bfloat16 [65536, 1024], P(('pin', 'board')), may hold values from -6 to 6
- slot_pin: int32 [128, 128, 16], P(('pin', 'board')), may hold values from 0 to 511
- slot_board: int32 [128, 128, 16], P(('pin', 'board')), may hold values from 0 to 255
- slot_walk: int32 [128, 128, 16], P(('pin', 'board')), may hold values from 1 to 32, as said below
- pair_count: int32 [128, 128], P(('pin', 'board')), may hold values from 1 to 16, as said below
Outputs:
- output: bfloat16 [65536, 1024], P(('pin', 'board'))
- grad_message: bfloat16 [2048, 1024], replicated
- grad_update: bfloat16 [1024, 1024], replicated
The draws below stay inside these ranges and needn't reach their ends.
Inputs may be any that keep to these rules, and one draw needn't show every extreme that they name: `slot_walk`: slots at or past their block's count hold arbitrary values in range. `pair_count`: in every draw some device receives 16 live slots from every device.
All inputs are finite; a program needn't handle non-finite values.
Results may differ from the reference program's by a relative error of at most 0.006.
The reference program's roundings to bfloat16 on the way (of `hidden`, `board_rows`, `neighbour`, `d_update`, `d_neighbour`, `slot_grad`, `message_grad` and `d_pre`) count: a program that leaves them out, or rounds other values in their place, can miss the bound.
Values may be sent and summed in bfloat16 or wider, within the bound.
A program may use at most 128 MiB of HBM per device.

```python
import jax
import jax.numpy as jnp
from jax import lax

F = 2048
H = 1024
PIN_DEV = 512
BOARD_DEV = 256
CAP = 16
PINS = 65536
BOARDS = 32768
DEVICES = 128


def draw_slot_pin(key, part):
    return jax.random.randint(jax.random.fold_in(key, 21), (DEVICES, DEVICES, CAP), 0, PIN_DEV, dtype=jnp.int32)


def draw_slot_board(key, part):
    return jax.random.randint(jax.random.fold_in(key, 22), (DEVICES, DEVICES, CAP), 0, BOARD_DEV, dtype=jnp.int32)


def draw_slot_walk(key, part):
    return jax.random.randint(jax.random.fold_in(key, 23), (DEVICES, DEVICES, CAP), 1, 33, dtype=jnp.int32)


def draw_pair_count(key, part):
    counts = jax.random.randint(jax.random.fold_in(key, 24), (DEVICES, DEVICES), 1, CAP + 1, dtype=jnp.int32)
    hot_owner = jax.random.randint(jax.random.fold_in(key, 25), (), 0, DEVICES, dtype=jnp.int32)
    column = jnp.arange(DEVICES, dtype=jnp.int32)[None, :]
    return jnp.where(column == hot_owner, CAP, counts).astype(jnp.int32)


def block_scale(rng, shape, cuts, low, largest):
    level, own = 1.0, jax.random.fold_in(rng, 6)
    for position, parts in cuts:
        steps = jnp.exp(jax.random.uniform(jax.random.fold_in(own, position), (parts,), jnp.float32, low / len(cuts), largest / len(cuts)))
        level = level * jnp.repeat(steps, shape[position] // parts).reshape([-1 if axis == position else 1 for axis in range(len(shape))])
    return level


def scatter_about(own_key, dims, deviation, bound, shards=(), kind=jnp.bfloat16):
    gain = block_scale(own_key, dims, shards, -0.22, 0.18) if shards else 1.0
    entries = jax.random.normal(own_key, dims, jnp.float32) * deviation * gain
    return jnp.minimum(jnp.maximum(entries, -bound), bound).astype(kind)


def setup_inputs(seed: int = 0) -> dict:
    key_list = jax.random.split(jax.random.key(seed), 9)
    features = scatter_about(key_list[0], (PINS, F), 1.0, 6.0, ((0, 128),))
    w_message = scatter_about(key_list[1], (F, H), F ** -0.5, 0.125)
    w_update = scatter_about(key_list[2], (H, H), (H // 4) ** -0.5, 0.375)
    cotangent = scatter_about(key_list[3], (PINS, H), 1.0, 6.0, ((0, 128),))
    slot_pin = draw_slot_pin(jax.random.fold_in(key_list[8], 71), 0)
    slot_board = draw_slot_board(jax.random.fold_in(key_list[8], 71), 0)
    slot_walk = draw_slot_walk(jax.random.fold_in(key_list[8], 71), 0)
    pair_count = draw_pair_count(jax.random.fold_in(key_list[8], 71), 0)
    return dict(features=features, w_message=w_message, w_update=w_update, cotangent=cotangent, slot_pin=slot_pin, slot_board=slot_board, slot_walk=slot_walk, pair_count=pair_count)


def silu_slope(value):
    sig = jax.nn.sigmoid(value)
    return sig * (1.0 + value * (1.0 - sig))


def reference(features, w_message, w_update, cotangent, slot_pin, slot_board, slot_walk, pair_count):
    slot_index = jnp.arange(CAP, dtype=jnp.int32)
    is_live = slot_index[None, None, :] < pair_count[:, :, None]
    walks = jnp.where(is_live, slot_walk, 0).astype(jnp.float32).reshape(-1)
    source = jnp.arange(DEVICES, dtype=jnp.int32)
    pin_ids = (slot_pin + source[:, None, None] * PIN_DEV).astype(jnp.int32).reshape(-1)
    board_ids = (slot_board + source[None, :, None] * BOARD_DEV).astype(jnp.int32).reshape(-1)
    pre_act = jnp.dot(features, w_message, preferred_element_type=jnp.float32)
    hidden = jax.nn.silu(pre_act).astype(jnp.bfloat16)
    board_degree = jax.ops.segment_sum(walks, board_ids, num_segments=BOARDS)
    board_total = jax.ops.segment_sum(walks[:, None] * hidden[pin_ids].astype(jnp.float32), board_ids, num_segments=BOARDS)
    board_rows = (board_total / jnp.maximum(board_degree, 1.0)[:, None]).astype(jnp.bfloat16)
    pin_degree = jax.ops.segment_sum(walks, pin_ids, num_segments=PINS)
    neigh_total = jax.ops.segment_sum(walks[:, None] * board_rows[board_ids].astype(jnp.float32), pin_ids, num_segments=PINS)
    neighbour = (neigh_total / jnp.maximum(pin_degree, 1.0)[:, None]).astype(jnp.bfloat16)
    update = jnp.dot(neighbour, w_update, preferred_element_type=jnp.float32)
    output = (hidden.astype(jnp.float32) + jax.nn.silu(update)).astype(jnp.bfloat16)
    d_update = (cotangent.astype(jnp.float32) * silu_slope(update)).astype(jnp.bfloat16)
    grad_update = lax.dot_general(neighbour, d_update, (((0,), (0,)), ((), ())), preferred_element_type=jnp.float32)
    d_neighbour = lax.dot_general(d_update, w_update, (((1,), (1,)), ((), ())), preferred_element_type=jnp.float32).astype(jnp.bfloat16)
    slot_scale = walks / jnp.maximum(pin_degree[pin_ids], 1.0)
    slot_grad = (slot_scale[:, None] * d_neighbour[pin_ids].astype(jnp.float32)).astype(jnp.bfloat16)
    board_grad = jax.ops.segment_sum(slot_grad.astype(jnp.float32), board_ids, num_segments=BOARDS) / jnp.maximum(board_degree, 1.0)[:, None]
    message_grad = (walks[:, None] * board_grad[board_ids]).astype(jnp.bfloat16)
    hidden_grad = cotangent.astype(jnp.float32) + jax.ops.segment_sum(message_grad.astype(jnp.float32), pin_ids, num_segments=PINS)
    d_pre = (hidden_grad * silu_slope(pre_act)).astype(jnp.bfloat16)
    grad_message = lax.dot_general(features, d_pre, (((0,), (0,)), ((), ())), preferred_element_type=jnp.float32)
    return output, grad_message.astype(jnp.bfloat16), grad_update.astype(jnp.bfloat16)
```

```python
import jax
import jax.numpy as jnp
from jax import lax
from jax.experimental import pallas as pl
from jax.experimental.pallas import tpu as pltpu
from jax.sharding import PartitionSpec as P

MESH = pl.DeviceIdType.MESH


def peer_of(step):
    pin = lax.axis_index("pin")
    board = lax.axis_index("board")
    dz, dx, dc, dy = step // 32, (step // 8) % 4, (step // 4) % 2, step % 4
    z, x, c = pin // 8, (pin // 2) % 4, pin % 2
    peer_pin = ((z + dz) % 4) * 8 + ((x + dx) % 4) * 2 + (c + dc) % 2
    return peer_pin, (board + dy) % 4


def exchange_kernel(x_ref, o_ref, send_sem, recv_sem, own_sem):
    me = lax.axis_index("pin") * 4 + lax.axis_index("board")
    barrier = pltpu.get_barrier_semaphore()

    @pl.loop(1, 128)
    def _(step):
        pl.semaphore_signal(barrier, inc=1, device_id=peer_of(step), device_id_type=MESH)

    pl.semaphore_wait(barrier, 127)
    own = pltpu.make_async_copy(x_ref.at[me], o_ref.at[me], own_sem)
    own.start()

    @pl.loop(1, 128)
    def _(step):
        pin, board = peer_of(step)
        pltpu.make_async_remote_copy(
            x_ref.at[pin * 4 + board],
            o_ref.at[me],
            send_sem,
            recv_sem,
            device_id=(pin, board),
            device_id_type=MESH,
        ).start()

    own.wait()
    part = pl.ds(0, 127)
    pltpu.make_async_copy(x_ref.at[part], x_ref.at[part], send_sem).wait()
    pltpu.make_async_copy(o_ref.at[part], o_ref.at[part], recv_sem).wait()


def exchange(x):
    return pl.pallas_call(
        exchange_kernel,
        out_shape=jax.ShapeDtypeStruct(x.shape, x.dtype),
        in_specs=[pl.BlockSpec(memory_space=pl.ANY)],
        out_specs=pl.BlockSpec(memory_space=pl.ANY),
        scratch_shapes=[pltpu.SemaphoreType.DMA] * 3,
        compiler_params=pltpu.CompilerParams(collective_id=0, has_side_effects=True),
    )(x)


def silu_slope(value):
    sig = jax.nn.sigmoid(value)
    return sig * (1.0 + value * (1.0 - sig))


def body(features, w_message, w_update, cotangent, slot_pin, slot_board, slot_walk, pair_count):
    pin_count = lax.axis_size("pin")
    board_count = lax.axis_size("board")
    devices_all = pin_count * board_count
    slots = slot_pin.shape[2]
    pin_rows = features.shape[0]
    board_rows_dev = pin_rows // 2
    width = w_message.shape[1]
    slot_index = jnp.arange(slots, dtype=jnp.int32)
    is_live = slot_index[None, :] < pair_count[0][:, None]
    walks_int = jnp.where(is_live, slot_walk[0], 0)
    walks_flat = walks_int.reshape(-1).astype(jnp.float32)
    pins_flat = slot_pin[0].reshape(-1)
    pre_act = jnp.dot(features, w_message, preferred_element_type=jnp.float32)
    hidden = jax.nn.silu(pre_act).astype(jnp.bfloat16)
    messages = jnp.take(hidden, pins_flat, axis=0).reshape(devices_all, slots, width)
    boards_sent = slot_board[0]
    recv_messages, recv_boards, recv_walks = (
        exchange(messages),
        lax.all_to_all(boards_sent, ("pin", "board"), split_axis=0, concat_axis=0, tiled=True),
        lax.all_to_all(walks_int, ("pin", "board"), split_axis=0, concat_axis=0, tiled=True),
    )
    recv_board_flat = recv_boards.reshape(-1)
    recv_weight = recv_walks.reshape(-1).astype(jnp.float32)
    board_match = jnp.arange(board_rows_dev, dtype=jnp.int32)[:, None] == recv_board_flat[None, :]
    board_weights = jnp.where(board_match, recv_weight[None, :], 0.0)
    board_degree = jnp.sum(board_weights, axis=1)
    board_total = jnp.dot(
        board_weights.astype(jnp.bfloat16),
        recv_messages.reshape(-1, width),
        preferred_element_type=jnp.float32,
    )
    board_rows = (board_total / jnp.maximum(board_degree, 1.0)[:, None]).astype(jnp.bfloat16)
    returned = jnp.take(board_rows, recv_board_flat, axis=0).reshape(devices_all, slots, width)
    read_rows = exchange(returned)
    pin_match = jnp.arange(pin_rows, dtype=jnp.int32)[:, None] == pins_flat[None, :]
    pin_weights = jnp.where(pin_match, walks_flat[None, :], 0.0)
    pin_degree = jnp.sum(pin_weights, axis=1)
    neigh_total = jnp.dot(
        pin_weights.astype(jnp.bfloat16),
        read_rows.reshape(-1, width),
        preferred_element_type=jnp.float32,
    )
    neighbour = (neigh_total / jnp.maximum(pin_degree, 1.0)[:, None]).astype(jnp.bfloat16)
    update = jnp.dot(neighbour, w_update, preferred_element_type=jnp.float32)
    output = (hidden.astype(jnp.float32) + jax.nn.silu(update)).astype(jnp.bfloat16)
    d_update = (cotangent.astype(jnp.float32) * silu_slope(update)).astype(jnp.bfloat16)
    grad_update = lax.dot_general(
        neighbour, d_update, (((0,), (0,)), ((), ())), preferred_element_type=jnp.float32
    )
    d_neighbour = lax.dot_general(
        d_update, w_update, (((1,), (1,)), ((), ())), preferred_element_type=jnp.float32
    ).astype(jnp.bfloat16)
    slot_scale = walks_flat / jnp.maximum(jnp.take(pin_degree, pins_flat, axis=0), 1.0)
    slot_grad = (
        slot_scale[:, None] * jnp.take(d_neighbour, pins_flat, axis=0).astype(jnp.float32)
    ).astype(jnp.bfloat16)
    slot_grad = slot_grad.reshape(devices_all, slots, width)
    recv_grads = exchange(slot_grad)
    board_sum = jnp.dot(
        board_match.astype(jnp.bfloat16),
        recv_grads.reshape(-1, width),
        preferred_element_type=jnp.float32,
    )
    board_grad = board_sum / jnp.maximum(board_degree, 1.0)[:, None]
    message_grad = (recv_weight[:, None] * jnp.take(board_grad, recv_board_flat, axis=0)).astype(
        jnp.bfloat16
    )
    message_grad = message_grad.reshape(devices_all, slots, width)
    back_grads = exchange(message_grad)
    neigh_grad = jnp.dot(
        pin_match.astype(jnp.bfloat16),
        back_grads.reshape(-1, width),
        preferred_element_type=jnp.float32,
    )
    hidden_grad = cotangent.astype(jnp.float32) + neigh_grad
    d_pre = (hidden_grad * silu_slope(pre_act)).astype(jnp.bfloat16)
    grad_message = lax.dot_general(
        features, d_pre, (((0,), (0,)), ((), ())), preferred_element_type=jnp.float32
    )
    total_message, total_update = lax.psum((grad_message, grad_update), ("pin", "board"))
    return (output, total_message.astype(jnp.bfloat16), total_update.astype(jnp.bfloat16))


def solution(mesh):
    in_specs = (
        P(("pin", "board"), None),
        P(),
        P(),
        P(("pin", "board"), None),
        P(("pin", "board"), None, None),
        P(("pin", "board"), None, None),
        P(("pin", "board"), None, None),
        P(("pin", "board"), None),
    )
    out_specs = (P(("pin", "board"), None), P(), P())
    return jax.shard_map(body, mesh=mesh, in_specs=in_specs, out_specs=out_specs, check_vma=False)
```

```python
import jax
import jax.numpy as jnp
from jax import lax
from jax.experimental import pallas as pl
from jax.experimental.pallas import tpu as pltpu
from jax.sharding import PartitionSpec as P

MESH = pl.DeviceIdType.MESH
BF = jnp.bfloat16
F32 = jnp.float32
DEV = 128
CAP = 16
SLOTS = DEV * CAP
PINS = 512
BOARDS = 256
F = 2048
H = 1024
W = 256
C = H // W
TILE = 512


def silu_slope(value):
    sig = jax.nn.sigmoid(value)
    return sig * (1.0 + value * (1.0 - sig))


def mm(a, b, dims=((1,), (0,))):
    return lax.dot_general(a, b, (dims, ((), ())), preferred_element_type=F32)


def iota(shape, axis):
    return lax.broadcasted_iota(jnp.int32, shape, axis)


def peer_of(step):
    pin = lax.axis_index("pin")
    board = lax.axis_index("board")
    dz = step % 4
    dx = (step // 4 + dz) % 4
    dy = (step // 16 + dx + dz) % 4
    dc = step // 64
    z, x, c = pin // 8, (pin // 2) % 4, pin % 2
    return ((z + dz) % 4) * 8 + ((x + dx) % 4) * 2 + (c + dc) % 2, (board + dy) % 4


def to_column(table):
    pick = (iota((SLOTS, DEV), 0) // CAP == iota((SLOTS, DEV), 1)).astype(F32).astype(BF)
    rows = mm(pick, table.astype(BF))
    keep = iota((SLOTS, DEV), 0) % CAP == iota((SLOTS, DEV), 1)
    return jnp.sum(jnp.where(keep, rows, 0.0), axis=1, keepdims=True)


def to_row(table):
    pick = (iota((DEV, SLOTS), 1) % CAP == iota((DEV, SLOTS), 0)).astype(F32).astype(BF)
    columns = mm(table.astype(BF), pick)
    keep = iota((DEV, SLOTS), 1) // CAP == iota((DEV, SLOTS), 0)
    return jnp.sum(jnp.where(keep, columns, 0.0), axis=0, keepdims=True)


def main_kernel(
    feat_hbm, wm_hbm, wu_hbm, cot_hbm, spin_ref, sboard_ref, swalk_ref, count_ref,
    out_hbm, gm_hbm, gu_hbm,
    feat, wm, wu, cot, out, gm, gu,
    pre, hid, s0, s1, ra, rb,
    pin_t, pin_m, pin_w, brd_t, brd_m, brd_w, feat_t,
    upd, dupd, nb, nb_t, scale_col, walk_col, pdeg, bdeg, brow_buf,
    table, idx_s, idx_r,
    load_sem, store_sem, idx_sem, send_sem, recv_sem,
):
    me = lax.axis_index("pin") * 4 + lax.axis_index("board")
    barrier = pltpu.get_barrier_semaphore()

    loads = [
        pltpu.make_async_copy(feat_hbm, feat, load_sem.at[0]),
        pltpu.make_async_copy(wm_hbm, wm, load_sem.at[1]),
        pltpu.make_async_copy(wu_hbm, wu, load_sem.at[2]),
        pltpu.make_async_copy(cot_hbm, cot, load_sem.at[3]),
    ]
    for load in loads:
        load.start()

    @pl.loop(1, DEV)
    def _(step):
        pl.semaphore_signal(barrier, inc=1, device_id=peer_of(step), device_id_type=MESH)

    diag = iota((DEV, DEV), 0) == iota((DEV, DEV), 1)
    count_col = jnp.sum(
        jnp.where(diag, jnp.broadcast_to(count_ref[...].astype(F32), (DEV, DEV)), 0.0), axis=1, keepdims=True
    )
    live = iota((DEV, CAP), 1).astype(F32) < count_col
    walks = jnp.where(live, swalk_ref[...], 0)
    table[...] = jnp.zeros_like(table)
    table[:, :CAP] = walks * 256 + sboard_ref[...]

    @pl.loop(0, DEV)
    def _(row):
        idx_s[row] = table[pl.ds(row, 1), :]

    table[...] = jnp.zeros_like(table)
    table[:, :CAP] = walks * 512 + spin_ref[...]
    packed = table[...]
    pin_hi = ((packed // 256) % 2).astype(F32)
    pin_lo = (packed % 256).astype(F32)
    walk_tab = (packed // 512).astype(F32)
    pin_col = to_column(pin_hi) * 256.0 + to_column(pin_lo)
    pin_t[...] = (iota((SLOTS, PINS), 1).astype(F32) == pin_col).astype(F32).astype(BF)

    pl.semaphore_wait(barrier, DEV - 1)

    own_idx = pltpu.make_async_copy(idx_s.at[me], idx_r.at[me], idx_sem.at[1])
    own_idx.start()

    @pl.loop(1, DEV)
    def _(step):
        pin, board = peer_of(step)
        pltpu.make_async_remote_copy(
            idx_s.at[pin * 4 + board], idx_r.at[me], idx_sem.at[0], idx_sem.at[1],
            device_id=(pin, board), device_id_type=MESH,
        ).start()

    def block(device):
        return pl.ds(pl.multiple_of(device * CAP, CAP), CAP)

    def send(phase, c, src, dst):
        pltpu.make_async_copy(src.at[c, block(me)], dst.at[c, block(me)], recv_sem.at[phase, c]).start()

        @pl.loop(1, DEV)
        def _(step):
            pin, board = peer_of(step)
            pltpu.make_async_remote_copy(
                src.at[c, block(pin * 4 + board)], dst.at[c, block(me)],
                send_sem.at[phase, c], recv_sem.at[phase, c],
                device_id=(pin, board), device_id_type=MESH,
            ).start()

    def wait_sent(phase, c, src):
        part = src.at[c, pl.ds(0, (DEV - 1) * CAP)]
        pltpu.make_async_copy(part, part, send_sem.at[phase, c]).wait()

    def wait_received(phase, c, dst):
        pltpu.make_async_copy(dst.at[c], dst.at[c], recv_sem.at[phase, c]).wait()

    def cols(c):
        return pl.ds(pl.multiple_of(c * W, W), W)

    def tile(i):
        return pl.ds(pl.multiple_of(i * TILE, TILE), TILE)

    loads[0].wait()
    loads[1].wait()

    @pl.loop(0, C)
    def _(c):
        value = mm(feat[...], wm[:, cols(c)])
        pre[:, cols(c)] = value
        hidden = (value * jax.nn.sigmoid(value)).astype(BF)
        hid[:, cols(c)] = hidden

        @pl.loop(0, SLOTS // TILE)
        def _(i):
            s0[c, tile(i)] = mm(pin_t[tile(i), :], hid[:, cols(c)]).astype(BF)

        send(0, c, s0, ra)

    pin_row = to_row(pin_hi) * 256.0 + to_row(pin_lo)
    walk_row = to_row(walk_tab)
    match = iota((PINS, SLOTS), 0).astype(F32) == pin_row
    pin_m[...] = match.astype(F32).astype(BF)
    weights = jnp.where(match, walk_row, 0.0)
    pin_w[...] = weights.astype(BF)
    pdeg[...] = jnp.maximum(jnp.sum(weights, axis=1, keepdims=True), 1.0)
    own_walk = to_column(walk_tab)
    degree_row = jnp.sum(pin_t[...].astype(F32) * own_walk, axis=0, keepdims=True)
    slot_degree = jnp.sum(pin_t[...].astype(F32) * degree_row, axis=1, keepdims=True)
    scale_col[...] = own_walk / jnp.maximum(slot_degree, 1.0)
    feat_t[...] = feat[...].T

    pltpu.make_async_copy(idx_r, idx_r, idx_sem.at[1]).wait()
    sent_idx = idx_s.at[pl.ds(0, DEV - 1)]
    pltpu.make_async_copy(sent_idx, sent_idx, idx_sem.at[0]).wait()

    @pl.loop(0, DEV)
    def _(row):
        table[pl.ds(row, 1), :] = idx_r[row]

    received = table[...]
    brd_tab = (received % 256).astype(F32)
    bwalk_tab = (received // 256).astype(F32)
    brd_t[...] = (iota((SLOTS, BOARDS), 1).astype(F32) == to_column(brd_tab)).astype(F32).astype(BF)
    walk_col[...] = to_column(bwalk_tab)
    match = iota((BOARDS, SLOTS), 0).astype(F32) == to_row(brd_tab)
    brd_m[...] = match.astype(F32).astype(BF)
    weights = jnp.where(match, to_row(bwalk_tab), 0.0)
    brd_w[...] = weights.astype(BF)
    bdeg[...] = jnp.maximum(jnp.sum(weights, axis=1, keepdims=True), 1.0)

    @pl.loop(0, C)
    def _(c):
        wait_received(0, c, ra)
        brow_buf[0] = (mm(brd_w[...], ra[c]) / bdeg[...]).astype(BF)

        @pl.loop(0, SLOTS // TILE)
        def _(i):
            s1[c, tile(i)] = mm(brd_t[tile(i), :], brow_buf[0]).astype(BF)

        send(1, c, s1, rb)

    loads[2].wait()
    loads[3].wait()
    upd[...] = jnp.zeros_like(upd)

    @pl.loop(0, C)
    def _(c):
        wait_received(1, c, rb)
        part = (mm(pin_w[...], rb[c]) / pdeg[...]).astype(BF)
        nb[:, cols(c)] = part

        @pl.loop(0, C)
        def _(n):
            upd[:, cols(n)] += mm(nb[:, cols(c)], wu[cols(c), cols(n)])

    @pl.loop(0, C)
    def _(n):
        update = upd[:, cols(n)]
        out[:, cols(n)] = (hid[:, cols(n)].astype(F32) + update * jax.nn.sigmoid(update)).astype(BF)
        dupd[:, cols(n)] = (cot[:, cols(n)].astype(F32) * silu_slope(update)).astype(BF)

    @pl.loop(0, C)
    def _(c):
        wait_sent(0, c, s0)
        brow_wide = mm(dupd[...], wu[cols(c), :], ((1,), (1,))).astype(BF)
        nb_t[0:PINS, 0:W] = brow_wide

        @pl.loop(0, SLOTS // TILE)
        def _(i):
            s0[c, tile(i)] = (scale_col[tile(i), :] * mm(pin_t[tile(i), :], nb_t[0:PINS, 0:W])).astype(BF)

        send(2, c, s0, ra)

    store_out = pltpu.make_async_copy(out, out_hbm, store_sem.at[0])
    store_out.start()
    nb_t[...] = nb[...].T

    @pl.loop(0, C)
    def _(n):
        gu[cols(n), :] = mm(nb_t[cols(n), :], dupd[...]).astype(BF)

    store_gu = pltpu.make_async_copy(gu, gu_hbm, store_sem.at[1])
    store_gu.start()

    @pl.loop(0, C)
    def _(c):
        wait_received(2, c, ra)
        wait_sent(1, c, s1)
        board_grad = mm(brd_m[...], ra[c]) / bdeg[...]
        high = board_grad.astype(BF)
        brow_buf[0] = high
        brow_buf[1] = (board_grad - high.astype(F32)).astype(BF)

        @pl.loop(0, SLOTS // TILE)
        def _(i):
            pick = brd_t[tile(i), :]
            rows = mm(pick, brow_buf[0]) + mm(pick, brow_buf[1])
            s1[c, tile(i)] = (walk_col[tile(i), :] * rows).astype(BF)

        send(3, c, s1, rb)

    @pl.loop(0, C)
    def _(c):
        wait_received(3, c, rb)
        grad = cot[:, cols(c)].astype(F32) + mm(pin_m[...], rb[c])
        d_pre = (grad * silu_slope(pre[:, cols(c)])).astype(BF)
        dupd[:, 0:W] = d_pre

        @pl.loop(0, F // TILE)
        def _(i):
            gm[tile(i), cols(c)] = mm(feat_t[tile(i), :], dupd[:, 0:W]).astype(BF)

    store_gm = pltpu.make_async_copy(gm, gm_hbm, store_sem.at[2])
    store_gm.start()

    @pl.loop(0, C)
    def _(c):
        wait_sent(2, c, s0)
        wait_sent(3, c, s1)

    store_out.wait()
    store_gu.wait()
    store_gm.wait()


def body(features, w_message, w_update, cotangent, slot_pin, slot_board, slot_walk, pair_count):
    hbm = pl.BlockSpec(memory_space=pl.ANY)
    vmem = pl.BlockSpec(memory_space=pltpu.VMEM)
    sem = pltpu.SemaphoreType.DMA
    output, gm, gu = pl.pallas_call(
        main_kernel,
        out_shape=(
            jax.ShapeDtypeStruct((PINS, H), BF),
            jax.ShapeDtypeStruct((F, H), BF),
            jax.ShapeDtypeStruct((H, H), BF),
        ),
        in_specs=[hbm] * 4 + [vmem] * 4,
        out_specs=(hbm, hbm, hbm),
        scratch_shapes=[
            pltpu.VMEM((PINS, F), BF), pltpu.VMEM((F, H), BF), pltpu.VMEM((H, H), BF), pltpu.VMEM((PINS, H), BF),
            pltpu.VMEM((PINS, H), BF), pltpu.VMEM((F, H), BF), pltpu.VMEM((H, H), BF),
            pltpu.VMEM((PINS, H), F32), pltpu.VMEM((PINS, H), BF),
            pltpu.VMEM((C, SLOTS, W), BF), pltpu.VMEM((C, SLOTS, W), BF),
            pltpu.VMEM((C, SLOTS, W), BF), pltpu.VMEM((C, SLOTS, W), BF),
            pltpu.VMEM((SLOTS, PINS), BF), pltpu.VMEM((PINS, SLOTS), BF), pltpu.VMEM((PINS, SLOTS), BF),
            pltpu.VMEM((SLOTS, BOARDS), BF), pltpu.VMEM((BOARDS, SLOTS), BF), pltpu.VMEM((BOARDS, SLOTS), BF),
            pltpu.VMEM((F, PINS), BF),
            pltpu.VMEM((PINS, H), F32), pltpu.VMEM((PINS, H), BF), pltpu.VMEM((PINS, H), BF), pltpu.VMEM((H, PINS), BF),
            pltpu.VMEM((SLOTS, 1), F32), pltpu.VMEM((SLOTS, 1), F32), pltpu.VMEM((PINS, 1), F32), pltpu.VMEM((BOARDS, 1), F32),
            pltpu.VMEM((2, BOARDS, W), BF),
            pltpu.VMEM((DEV, DEV), jnp.int32), pltpu.VMEM((DEV, 1, DEV), jnp.int32), pltpu.VMEM((DEV, 1, DEV), jnp.int32),
            sem((4,)), sem((3,)), sem((2,)), sem((4, C)), sem((4, C)),
        ],
        name="layer",
        compiler_params=pltpu.CompilerParams(
            collective_id=0, has_side_effects=True, vmem_limit_bytes=62 * 1024 * 1024
        ),
    )(
        features, w_message, w_update, cotangent,
        slot_pin[0], slot_board[0], slot_walk[0], pair_count,
    )
    wide = lax.optimization_barrier((gm.astype(F32), gu.astype(F32)))
    total_message, total_update = lax.psum(wide, ("pin", "board"))
    return (output, total_message.astype(BF), total_update.astype(BF))


def solution(mesh):
    in_specs = (
        P(("pin", "board"), None),
        P(),
        P(),
        P(("pin", "board"), None),
        P(("pin", "board"), None, None),
        P(("pin", "board"), None, None),
        P(("pin", "board"), None, None),
        P(("pin", "board"), None),
    )
    out_specs = (P(("pin", "board"), None), P(), P())
    return jax.shard_map(body, mesh=mesh, in_specs=in_specs, out_specs=out_specs, check_vma=False)
```

```python
import jax
import jax.numpy as jnp
from jax import lax
from jax.experimental import pallas as pl
from jax.experimental.pallas import tpu as pltpu
from jax.sharding import PartitionSpec as P

MESH = pl.DeviceIdType.MESH
BF = jnp.bfloat16
F32 = jnp.float32
DEV = 128
CAP = 16
SLOTS = DEV * CAP
PINS = 512
BOARDS = 256
F = 2048
H = 1024
W = 256
C = H // W
TILE = 512


def silu_slope(value):
    sig = jax.nn.sigmoid(value)
    return sig * (1.0 + value * (1.0 - sig))


def mm(a, b, dims=((1,), (0,))):
    return lax.dot_general(a, b, (dims, ((), ())), preferred_element_type=F32)


def iota(shape, axis):
    return lax.broadcasted_iota(jnp.int32, shape, axis)


def peer_of(step):
    pin = lax.axis_index("pin")
    board = lax.axis_index("board")
    dz = step % 4
    dx = (step // 4 + dz) % 4
    dy = (step // 16 + dx + dz) % 4
    dc = step // 64
    z, x, c = pin // 8, (pin // 2) % 4, pin % 2
    return ((z + dz) % 4) * 8 + ((x + dx) % 4) * 2 + (c + dc) % 2, (board + dy) % 4


def relative(axis, step):
    pin = lax.axis_index("pin")
    place = [pin // 8, (pin // 2) % 4, lax.axis_index("board")]
    if isinstance(step, int):
        place[axis] = (place[axis] + step) % 4
    else:
        b, d = (axis + 1) % 3, (axis + 2) % 3
        place[b] = (place[b] + step // 4) % 4
        place[d] = (place[d] + step) % 4
        rank = place[b] * 4 + place[d]
        return (place[0] * 8 + place[1] * 2 + pin % 2, place[2]), rank
    return (place[0] * 8 + place[1] * 2 + pin % 2, place[2]), place[axis]


def grad_steps(src, dst, row0, c, buf, brow0, axis, send_sem, recv_sem):
    pin = lax.axis_index("pin")
    core = pin % 2
    partner = (pin + 1 - 2 * core, lax.axis_index("board"))
    quarter = relative(axis, 0)[1]
    rank = relative(axis, jnp.int32(0))[1]
    half = W // 2
    own = pl.ds(pl.multiple_of(c * W + core * half, half), half)
    other = pl.ds(pl.multiple_of(c * W + (1 - core) * half, half), half)
    left, right = pl.ds(0, half), pl.ds(half, half)
    every = pl.ds(row0, 1024)
    pair_buf = buf.at[pl.ds(brow0, 1024), left]
    line_buf = buf.at[pl.ds(brow0, 768), right]
    plane_buf = buf.at[pl.ds(brow0 + 768, 240), right]

    def line_rows(q):
        return pl.ds(pl.multiple_of(row0 + q * 256, 256), 256)

    def plane_rows(r):
        return pl.ds(pl.multiple_of(row0 + quarter * 256 + r * 16, 16), 16)

    def put(a, b, step, device):
        pltpu.make_async_remote_copy(
            a, b, send_sem.at[step], recv_sem.at[step], device_id=device, device_id_type=MESH
        ).start()

    def arrived(like, step):
        pltpu.make_async_copy(like, like, recv_sem.at[step]).wait()

    def pair_out():
        put(src.at[every, other], pair_buf, 0, partner)

    def line_out():
        arrived(pair_buf, 0)
        src[every, own] = (src[every, own].astype(F32) + pair_buf[...].astype(F32)).astype(BF)
        for dq in (1, 3, 2):
            device, q = relative(axis, dq)
            put(src.at[line_rows(q), own], buf.at[pl.ds(brow0 + (dq - 1) * 256, 256), right], 1, device)

    def plane_out():
        arrived(line_buf, 1)
        total = src[line_rows(quarter), own].astype(F32)
        for i in range(3):
            total += buf[brow0 + i * 256:brow0 + (i + 1) * 256, half:].astype(F32)
        src[line_rows(quarter), own] = total.astype(BF)

        @pl.loop(1, 16)
        def _(step):
            device, r = relative(axis, step)
            put(
                src.at[plane_rows(r), own],
                buf.at[pl.ds(pl.multiple_of(brow0 + 752 + step * 16, 16), 16), right],
                2, device,
            )

    def plane_back():
        arrived(plane_buf, 2)
        parts = plane_buf[...].astype(F32).reshape(15, 16, half)
        total = src[plane_rows(rank), own].astype(F32) + jnp.sum(parts, axis=0)
        dst[plane_rows(rank), own] = total.astype(BF)

        @pl.loop(1, 16)
        def _(step):
            device, _ = relative(axis, step)
            piece = dst.at[plane_rows(rank), own]
            put(piece, piece, 3, device)

    def line_back():
        arrived(plane_buf, 3)
        piece = dst.at[line_rows(quarter), own]
        for dq in (1, 3, 2):
            put(piece, piece, 4, relative(axis, dq)[0])

    def pair_back():
        arrived(line_buf, 4)
        piece = dst.at[every, own]
        put(piece, piece, 5, partner)

    def finish():
        arrived(pair_buf, 5)

    def sent():
        for step, like in enumerate((pair_buf, line_buf, plane_buf, plane_buf, line_buf, pair_buf)):
            pltpu.make_async_copy(like, like, send_sem.at[step]).wait()

    return [pair_out, line_out, plane_out, plane_back, line_back, pair_back, finish, sent]


def to_column(table):
    pick = (iota((SLOTS, DEV), 0) // CAP == iota((SLOTS, DEV), 1)).astype(F32).astype(BF)
    rows = mm(pick, table.astype(BF))
    keep = iota((SLOTS, DEV), 0) % CAP == iota((SLOTS, DEV), 1)
    return jnp.sum(jnp.where(keep, rows, 0.0), axis=1, keepdims=True)


def to_row(table):
    pick = (iota((DEV, SLOTS), 1) % CAP == iota((DEV, SLOTS), 0)).astype(F32).astype(BF)
    columns = mm(table.astype(BF), pick)
    keep = iota((DEV, SLOTS), 1) // CAP == iota((DEV, SLOTS), 0)
    return jnp.sum(jnp.where(keep, columns, 0.0), axis=0, keepdims=True)


def main_kernel(
    feat_hbm, wm_hbm, wu_hbm, cot_hbm, spin_ref, sboard_ref, swalk_ref, count_ref,
    out, gm, gu,
    feat, wm, wu, cot,
    pre, hid, s0, s1, ra, rb,
    pin_t, pin_w, brd_t, brd_w, feat_t,
    upd, nb_t, scale_col, walk_col, pdeg, bdeg, brow_buf, grad_buf, small,
    table, idx_s, idx_r,
    load_sem, idx_sem, send_sem, recv_sem, gsend_sem, grecv_sem,
):
    me = lax.axis_index("pin") * 4 + lax.axis_index("board")
    barrier = pltpu.get_barrier_semaphore()

    loads = [
        pltpu.make_async_copy(feat_hbm, feat, load_sem.at[0]),
        pltpu.make_async_copy(wm_hbm, wm, load_sem.at[1]),
        pltpu.make_async_copy(wu_hbm, wu, load_sem.at[2]),
        pltpu.make_async_copy(cot_hbm, cot, load_sem.at[3]),
    ]
    for load in loads:
        load.start()

    @pl.loop(1, DEV)
    def _(step):
        pl.semaphore_signal(barrier, inc=1, device_id=peer_of(step), device_id_type=MESH)

    def block(device):
        return pl.ds(pl.multiple_of(device * CAP, CAP), CAP)

    def send(phase, c, src, dst):
        pltpu.make_async_copy(src.at[c, block(me)], dst.at[c, block(me)], recv_sem.at[phase, c]).start()

        @pl.loop(1, DEV)
        def _(step):
            pin, board = peer_of(step)
            pltpu.make_async_remote_copy(
                src.at[c, block(pin * 4 + board)], dst.at[c, block(me)],
                send_sem.at[phase, c], recv_sem.at[phase, c],
                device_id=(pin, board), device_id_type=MESH,
            ).start()

    def wait_sent(phase, c, src):
        part = src.at[c, pl.ds(0, (DEV - 1) * CAP)]
        pltpu.make_async_copy(part, part, send_sem.at[phase, c]).wait()

    def wait_received(phase, c, dst):
        pltpu.make_async_copy(dst.at[c], dst.at[c], recv_sem.at[phase, c]).wait()

    def cols(c):
        return pl.ds(pl.multiple_of(c * W, W), W)

    def tile(i):
        return pl.ds(pl.multiple_of(i * TILE, TILE), TILE)

    live = iota((CAP, DEV), 0) < count_ref[...]
    walks = jnp.where(live, swalk_ref[...], 0)
    table[...] = jnp.zeros_like(table)
    table[:CAP, :] = (walks * 512 + spin_ref[...]).astype(F32)
    packed = table[...].T.astype(jnp.int32)
    pin_hi = ((packed // 256) % 2).astype(F32)
    pin_lo = (packed % 256).astype(F32)
    walk_tab = (packed // 512).astype(F32)
    pin_col = to_column(pin_hi) * 256.0 + to_column(pin_lo)
    pin_t[...] = (iota((SLOTS, PINS), 1).astype(F32) == pin_col).astype(F32).astype(BF)
    loads[0].wait()
    loads[1].wait()

    def project(c):
        value = mm(feat[...], wm[:, cols(c)])
        pre[:, cols(c)] = value
        hid[:, cols(c)] = (value * jax.nn.sigmoid(value)).astype(BF)

        @pl.loop(0, SLOTS // TILE)
        def _(i):
            s0[c, tile(i)] = mm(pin_t[tile(i), :], hid[:, cols(c)]).astype(BF)

    project(0)
    pl.semaphore_wait(barrier, DEV - 1)
    send(0, 0, s0, ra)

    table[:CAP, :] = (walks * 256 + sboard_ref[...]).astype(F32)
    table[...] = table[...].T

    @pl.loop(0, DEV)
    def _(row):
        idx_s[row] = table[pl.ds(row, 1), :].astype(jnp.int32)

    pltpu.make_async_copy(idx_s.at[me], idx_r.at[me], idx_sem.at[1]).start()

    @pl.loop(1, DEV)
    def _(step):
        pin, board = peer_of(step)
        pltpu.make_async_remote_copy(
            idx_s.at[pin * 4 + board], idx_r.at[me], idx_sem.at[0], idx_sem.at[1],
            device_id=(pin, board), device_id_type=MESH,
        ).start()

    @pl.loop(1, C)
    def _(c):
        project(c)
        send(0, c, s0, ra)

    pin_row = to_row(pin_hi) * 256.0 + to_row(pin_lo)
    walk_row = to_row(walk_tab)
    match = iota((PINS, SLOTS), 0).astype(F32) == pin_row
    weights = jnp.where(match, walk_row, 0.0)
    pin_w[...] = weights.astype(BF)
    pdeg[...] = jnp.maximum(jnp.sum(weights, axis=1, keepdims=True), 1.0)
    own_walk = to_column(walk_tab)
    degree_row = jnp.sum(pin_t[...].astype(F32) * own_walk, axis=0, keepdims=True)
    slot_degree = jnp.sum(pin_t[...].astype(F32) * degree_row, axis=1, keepdims=True)
    scale_col[...] = own_walk / jnp.maximum(slot_degree, 1.0)
    feat_t[...] = feat[...].T

    pltpu.make_async_copy(idx_r, idx_r, idx_sem.at[1]).wait()
    sent_idx = idx_s.at[pl.ds(0, DEV - 1)]
    pltpu.make_async_copy(sent_idx, sent_idx, idx_sem.at[0]).wait()

    @pl.loop(0, DEV)
    def _(row):
        table[pl.ds(row, 1), :] = idx_r[row].astype(F32)

    received = table[...].astype(jnp.int32)
    brd_tab = (received % 256).astype(F32)
    bwalk_tab = (received // 256).astype(F32)
    brd_t[...] = (iota((SLOTS, BOARDS), 1).astype(F32) == to_column(brd_tab)).astype(F32).astype(BF)
    walk_col[...] = to_column(bwalk_tab)
    match = iota((BOARDS, SLOTS), 0).astype(F32) == to_row(brd_tab)
    weights = jnp.where(match, to_row(bwalk_tab), 0.0)
    brd_w[...] = weights.astype(BF)
    bdeg[...] = jnp.maximum(jnp.sum(weights, axis=1, keepdims=True), 1.0)

    @pl.loop(0, C)
    def _(c):
        wait_received(0, c, ra)
        brow_buf[0] = (mm(brd_w[...], ra[c]) / bdeg[...]).astype(BF)

        @pl.loop(0, SLOTS // TILE)
        def _(i):
            s1[c, tile(i)] = mm(brd_t[tile(i), :], brow_buf[0]).astype(BF)

        send(1, c, s1, rb)

    brd_w[...] = (brd_w[...].astype(F32) > 0.0).astype(F32).astype(BF)
    loads[2].wait()
    loads[3].wait()
    upd[...] = jnp.zeros_like(upd)

    @pl.loop(0, C)
    def _(c):
        wait_received(1, c, rb)
        part = (mm(pin_w[...], rb[c]) / pdeg[...]).astype(BF)
        small[...] = part
        nb_t[cols(c), :] = part.T

        @pl.loop(0, C)
        def _(n):
            upd[:, cols(n)] += mm(small[...], wu[cols(c), cols(n)])

    @pl.loop(0, C)
    def _(n):
        feat[:, cols(n)] = (cot[:, cols(n)].astype(F32) * silu_slope(upd[:, cols(n)])).astype(BF)

    @pl.loop(0, C)
    def _(c):
        wait_sent(0, c, s0)
        small[...] = mm(feat[:, :H], wu[cols(c), :], ((1,), (1,))).astype(BF)

        @pl.loop(0, SLOTS // TILE)
        def _(i):
            s0[c, tile(i)] = (scale_col[tile(i), :] * mm(pin_t[tile(i), :], small[...])).astype(BF)

        send(2, c, s0, ra)

    @pl.loop(0, C)
    def _(n):
        wu[cols(n), :] = mm(nb_t[cols(n), :], feat[:, :H]).astype(BF)

    update_steps = [
        grad_steps(wu, gu, 0, i, grad_buf.at[i // 2], (i % 2) * 1024, i % 3, gsend_sem.at[i], grecv_sem.at[i])
        for i in range(4)
    ]
    for steps in update_steps:
        steps[0]()

    @pl.loop(0, C)
    def _(n):
        update = upd[:, cols(n)]
        out[:, cols(n)] = (hid[:, cols(n)].astype(F32) + update * jax.nn.sigmoid(update)).astype(BF)

    pin_w[...] = (pin_w[...].astype(F32) > 0.0).astype(F32).astype(BF)

    for c in range(C):
        wait_received(2, c, ra)
        wait_sent(1, c, s1)
        board_grad = mm(brd_w[...], ra[c]) / bdeg[...]
        high = board_grad.astype(BF)
        brow_buf[0] = high
        brow_buf[1] = (board_grad - high.astype(F32)).astype(BF)

        @pl.loop(0, SLOTS // TILE)
        def _(i):
            pick = brd_t[tile(i), :]
            rows = mm(pick, brow_buf[0]) + mm(pick, brow_buf[1])
            s1[c, tile(i)] = (walk_col[tile(i), :] * rows).astype(BF)

        send(3, c, s1, rb)
        for steps in update_steps:
            steps[1 + c]()

    message_steps = []
    for c in range(C):
        wait_received(3, c, rb)
        grad = cot[:, cols(c)].astype(F32) + mm(pin_w[...], rb[c])
        small[...] = (grad * silu_slope(pre[:, cols(c)])).astype(BF)

        @pl.loop(0, F // TILE)
        def _(i):
            wm[tile(i), cols(c)] = mm(feat_t[tile(i), :], small[...]).astype(BF)

        message_steps.append([
            grad_steps(
                wm, gm, h * 1024, c, ra.at[c], h * 1024, (2 * c + h) % 3,
                gsend_sem.at[4 + 2 * c + h], grecv_sem.at[4 + 2 * c + h],
            )
            for h in range(2)
        ])
        if c < 2:
            for steps in update_steps:
                steps[5 + c]()
        for back in range(c + 1):
            for steps in message_steps[c - back]:
                steps[back]()

    for tick in range(1, 7):
        for back in range(tick, min(tick + C, 7)):
            for steps in message_steps[C - 1 + tick - back]:
                steps[back]()

    @pl.loop(0, C)
    def _(c):
        wait_sent(2, c, s0)
        wait_sent(3, c, s1)

    for steps in update_steps + message_steps[0] + message_steps[1] + message_steps[2] + message_steps[3]:
        steps[7]()


def body(features, w_message, w_update, cotangent, slot_pin, slot_board, slot_walk, pair_count):
    hbm = pl.BlockSpec(memory_space=pl.ANY)
    vmem = pl.BlockSpec(memory_space=pltpu.VMEM)
    sem = pltpu.SemaphoreType.DMA
    output, gm, gu = pl.pallas_call(
        main_kernel,
        out_shape=(
            jax.ShapeDtypeStruct((PINS, H), BF),
            jax.ShapeDtypeStruct((F, H), BF),
            jax.ShapeDtypeStruct((H, H), BF),
        ),
        in_specs=[hbm] * 4 + [vmem] * 4,
        out_specs=(vmem, vmem, vmem),
        scratch_shapes=[
            pltpu.VMEM((PINS, F), BF), pltpu.VMEM((F, H), BF), pltpu.VMEM((H, H), BF), pltpu.VMEM((PINS, H), BF),
            pltpu.VMEM((PINS, H), F32), pltpu.VMEM((PINS, H), BF),
            pltpu.VMEM((C, SLOTS, W), BF), pltpu.VMEM((C, SLOTS, W), BF),
            pltpu.VMEM((C, SLOTS, W), BF), pltpu.VMEM((C, SLOTS, W), BF),
            pltpu.VMEM((SLOTS, PINS), BF), pltpu.VMEM((PINS, SLOTS), BF),
            pltpu.VMEM((SLOTS, BOARDS), BF), pltpu.VMEM((BOARDS, SLOTS), BF),
            pltpu.VMEM((F, PINS), BF),
            pltpu.VMEM((PINS, H), F32), pltpu.VMEM((H, PINS), BF),
            pltpu.VMEM((SLOTS, 1), F32), pltpu.VMEM((SLOTS, 1), F32), pltpu.VMEM((PINS, 1), F32), pltpu.VMEM((BOARDS, 1), F32),
            pltpu.VMEM((2, BOARDS, W), BF), pltpu.VMEM((2, SLOTS, W), BF), pltpu.VMEM((PINS, W), BF),
            pltpu.VMEM((DEV, DEV), F32), pltpu.VMEM((DEV, 1, DEV), jnp.int32), pltpu.VMEM((DEV, 1, DEV), jnp.int32),
            sem((4,)), sem((2,)), sem((4, C)), sem((4, C)), sem((12, 6)), sem((12, 6)),
        ],
        name="layer",
        compiler_params=pltpu.CompilerParams(
            collective_id=0, has_side_effects=True, vmem_limit_bytes=62 * 1024 * 1024
        ),
    )(
        features, w_message, w_update, cotangent,
        slot_pin[0].T, slot_board[0].T, slot_walk[0].T, pair_count,
    )
    return output, gm, gu


def solution(mesh):
    in_specs = (
        P(("pin", "board"), None),
        P(),
        P(),
        P(("pin", "board"), None),
        P(("pin", "board"), None, None),
        P(("pin", "board"), None, None),
        P(("pin", "board"), None, None),
        P(("pin", "board"), None),
    )
    out_specs = (P(("pin", "board"), None), P(), P())
    return jax.shard_map(body, mesh=mesh, in_specs=in_specs, out_specs=out_specs, check_vma=False)
```

```python
import jax
import jax.numpy as jnp
from jax import lax
from jax.experimental import pallas as pl
from jax.experimental.pallas import tpu as pltpu
from jax.sharding import PartitionSpec as P

MESH = pl.DeviceIdType.MESH
BF = jnp.bfloat16
F32 = jnp.float32
DEV = 128
CAP = 16
SLOTS = DEV * CAP
PINS = 512
BOARDS = 256
F = 2048
H = 1024
W = 256
C = H // W
TILE = 512


def silu_slope(value):
    sig = jax.nn.sigmoid(value)
    return sig * (1.0 + value * (1.0 - sig))


def mm(a, b, dims=((1,), (0,))):
    return lax.dot_general(a, b, (dims, ((), ())), preferred_element_type=F32)


def iota(shape, axis):
    return lax.broadcasted_iota(jnp.int32, shape, axis)


def places():
    pin = lax.axis_index("pin")
    z, x, y = lax.div(pin, 8), lax.rem(lax.div(pin, 2), 4), lax.axis_index("board")
    zs = [lax.rem(z + i, 4) * 8 for i in range(4)]
    xs = [lax.rem(x + i, 4) * 2 for i in range(4)]
    ys = [lax.rem(y + i, 4) for i in range(4)]
    return zs, xs, lax.rem(pin, 2), ys


def for_peers(visit):
    zs, xs, core, ys = places()

    def group(step, first):
        dc, dy = lax.div(step, 4), lax.rem(step, 4)
        c = lax.rem(core + dc, 2)
        rows = [lax.rem(ys[i] + dy, 4) for i in range(4)]
        for i in range(4):
            for dz in range(4):
                if first and i == 0 and dz == 0:
                    continue
                dx = (i + dz) % 4
                visit((zs[dz] + xs[dx] + c, rows[(dx + dz) % 4]))

    group(jnp.int32(0), True)

    @pl.loop(1, 8)
    def _(step):
        group(step, False)


def line_of(axis):
    zs, xs, core, ys = places()
    tables, scale = [zs, xs, ys], (8, 2, 1)[axis]
    others = []
    for i in (1, 3, 2):
        place = [zs[0], xs[0], ys[0]]
        place[axis] = tables[axis][i]
        others.append(((place[0] + place[1] + core, place[2]), lax.div(place[axis], scale), i - 1))
    return lax.div(tables[axis][0], scale), others


def plane_of(axis):
    zs, xs, core, ys = places()
    tables, scales = [zs, xs, ys], (8, 2, 1)
    b, d = (axis + 1) % 3, (axis + 2) % 3
    rb = [lax.div(v, scales[b]) * 4 for v in tables[b]]
    rd = [lax.div(v, scales[d]) for v in tables[d]]
    others = []
    for i in range(4):
        for j in range(4):
            if i or j:
                k, m = i, (i + j) % 4
                if not (k or m):
                    continue
                place = [zs[0], xs[0], ys[0]]
                place[b], place[d] = tables[b][k], tables[d][m]
                others.append(((place[0] + place[1] + core, place[2]), rb[k] + rd[m], 4 * k + m - 1))
    return rb[0] + rd[0], others


def grad_steps(src, dst, row0, c, buf, brow0, axis, send_sem, recv_sem):
    pin = lax.axis_index("pin")
    core = lax.rem(pin, 2)
    partner = (pin + 1 - 2 * core, lax.axis_index("board"))
    quarter, line = line_of(axis)
    rank, plane = plane_of(axis)
    half = W // 2
    own = pl.ds(pl.multiple_of(c * W + core * half, half), half)
    other = pl.ds(pl.multiple_of(c * W + (1 - core) * half, half), half)
    left, right = pl.ds(0, half), pl.ds(half, half)
    every = pl.ds(row0, 1024)
    pair_buf = buf.at[pl.ds(brow0, 1024), left]
    line_buf = buf.at[pl.ds(brow0, 768), right]
    plane_buf = buf.at[pl.ds(brow0 + 768, 240), right]

    def line_rows(q):
        return pl.ds(pl.multiple_of(row0 + q * 256, 256), 256)

    def plane_rows(r):
        return pl.ds(pl.multiple_of(row0 + quarter * 256 + r * 16, 16), 16)

    def put(a, b, step, device):
        pltpu.make_async_remote_copy(
            a, b, send_sem.at[step], recv_sem.at[step], device_id=device, device_id_type=MESH
        ).start()

    def arrived(like, step):
        pltpu.make_async_copy(like, like, recv_sem.at[step]).wait()

    def pair_out():
        put(src.at[every, other], pair_buf, 0, partner)

    def line_out():
        arrived(pair_buf, 0)
        src[every, own] = (src[every, own].astype(F32) + pair_buf[...].astype(F32)).astype(BF)
        for device, q, slot in line:
            put(src.at[line_rows(q), own], buf.at[pl.ds(brow0 + slot * 256, 256), right], 1, device)

    def plane_out():
        arrived(line_buf, 1)
        total = src[line_rows(quarter), own].astype(F32)
        for i in range(3):
            total += buf[brow0 + i * 256:brow0 + (i + 1) * 256, half:].astype(F32)
        src[line_rows(quarter), own] = total.astype(BF)

        for device, r, slot in plane:
            put(src.at[plane_rows(r), own], buf.at[pl.ds(brow0 + 768 + slot * 16, 16), right], 2, device)

    def plane_back():
        arrived(plane_buf, 2)
        parts = plane_buf[...].astype(F32).reshape(15, 16, half)
        total = src[plane_rows(rank), own].astype(F32) + jnp.sum(parts, axis=0)
        dst[plane_rows(rank), own] = total.astype(BF)

        piece = dst.at[plane_rows(rank), own]
        for device, _, _ in plane:
            put(piece, piece, 3, device)

    def line_back():
        arrived(plane_buf, 3)
        piece = dst.at[line_rows(quarter), own]
        for device, _, _ in line:
            put(piece, piece, 4, device)

    def pair_back():
        arrived(line_buf, 4)
        piece = dst.at[every, own]
        put(piece, piece, 5, partner)

    def finish():
        arrived(pair_buf, 5)

    def sent():
        for step, like in enumerate((pair_buf, line_buf, plane_buf, plane_buf, line_buf, pair_buf)):
            pltpu.make_async_copy(like, like, send_sem.at[step]).wait()

    return [pair_out, line_out, plane_out, plane_back, line_back, pair_back, finish, sent]


def to_column(table):
    pick = (iota((SLOTS, DEV), 0) // CAP == iota((SLOTS, DEV), 1)).astype(F32).astype(BF)
    rows = mm(pick, table.astype(BF))
    keep = iota((SLOTS, DEV), 0) % CAP == iota((SLOTS, DEV), 1)
    return jnp.sum(jnp.where(keep, rows, 0.0), axis=1, keepdims=True)


def to_row(table):
    pick = (iota((DEV, SLOTS), 1) % CAP == iota((DEV, SLOTS), 0)).astype(F32).astype(BF)
    columns = mm(table.astype(BF), pick)
    keep = iota((DEV, SLOTS), 1) // CAP == iota((DEV, SLOTS), 0)
    return jnp.sum(jnp.where(keep, columns, 0.0), axis=0, keepdims=True)


def main_kernel(
    feat_hbm, wm_hbm, wu_hbm, cot_hbm, spin_ref, sboard_ref, swalk_ref, count_ref,
    out, gm, gu,
    feat, wm, wu, cot,
    pre, hid, s0, s1, ra, rb,
    pin_t, pin_w, brd_t, brd_w, feat_t,
    upd, nb_t, scale_col, walk_col, pdeg, bdeg, brow_buf, grad_buf, small,
    table, idx_s, idx_r,
    load_sem, idx_sem, send_sem, recv_sem, gsend_sem, grecv_sem,
):
    me = lax.axis_index("pin") * 4 + lax.axis_index("board")
    barrier = pltpu.get_barrier_semaphore()

    loads = [
        pltpu.make_async_copy(feat_hbm, feat, load_sem.at[0]),
        pltpu.make_async_copy(wm_hbm, wm, load_sem.at[1]),
        pltpu.make_async_copy(wu_hbm, wu, load_sem.at[2]),
        pltpu.make_async_copy(cot_hbm, cot, load_sem.at[3]),
    ]
    for load in loads:
        load.start()

    for_peers(lambda peer: pl.semaphore_signal(barrier, inc=1, device_id=peer, device_id_type=MESH))

    def block(device):
        return pl.ds(pl.multiple_of(device * CAP, CAP), CAP)

    def send(phase, c, src, dst):
        pltpu.make_async_copy(src.at[c, block(me)], dst.at[c, block(me)], recv_sem.at[phase, c]).start()

        def put(peer):
            pltpu.make_async_remote_copy(
                src.at[c, block(peer[0] * 4 + peer[1])], dst.at[c, block(me)],
                send_sem.at[phase, c], recv_sem.at[phase, c],
                device_id=peer, device_id_type=MESH,
            ).start()

        for_peers(put)

    def wait_sent(phase, c, src):
        part = src.at[c, pl.ds(0, (DEV - 1) * CAP)]
        pltpu.make_async_copy(part, part, send_sem.at[phase, c]).wait()

    def wait_received(phase, c, dst):
        pltpu.make_async_copy(dst.at[c], dst.at[c], recv_sem.at[phase, c]).wait()

    def cols(c):
        return pl.ds(pl.multiple_of(c * W, W), W)

    def tile(i):
        return pl.ds(pl.multiple_of(i * TILE, TILE), TILE)

    live = iota((CAP, DEV), 0) < count_ref[...]
    walks = jnp.where(live, swalk_ref[...], 0)
    table[...] = jnp.zeros_like(table)
    table[:CAP, :] = (walks * 512 + spin_ref[...]).astype(F32)
    packed = table[...].T.astype(jnp.int32)
    pin_hi = ((packed // 256) % 2).astype(F32)
    pin_lo = (packed % 256).astype(F32)
    walk_tab = (packed // 512).astype(F32)
    pin_col = to_column(pin_hi) * 256.0 + to_column(pin_lo)
    pin_t[...] = (iota((SLOTS, PINS), 1).astype(F32) == pin_col).astype(F32).astype(BF)
    loads[0].wait()
    loads[1].wait()

    def project(c):
        value = mm(feat[...], wm[:, cols(c)])
        pre[:, cols(c)] = value
        hid[:, cols(c)] = (value * jax.nn.sigmoid(value)).astype(BF)

        @pl.loop(0, SLOTS // TILE)
        def _(i):
            s0[c, tile(i)] = mm(pin_t[tile(i), :], hid[:, cols(c)]).astype(BF)

    project(0)
    pl.semaphore_wait(barrier, DEV - 1)
    send(0, 0, s0, ra)

    table[:CAP, :] = (walks * 256 + sboard_ref[...]).astype(F32)
    table[...] = table[...].T

    @pl.loop(0, DEV)
    def _(row):
        idx_s[row] = table[pl.ds(row, 1), :].astype(jnp.int32)

    pltpu.make_async_copy(idx_s.at[me], idx_r.at[me], idx_sem.at[1]).start()

    def put_table(peer):
        pltpu.make_async_remote_copy(
            idx_s.at[peer[0] * 4 + peer[1]], idx_r.at[me], idx_sem.at[0], idx_sem.at[1],
            device_id=peer, device_id_type=MESH,
        ).start()

    for_peers(put_table)

    @pl.loop(1, C)
    def _(c):
        project(c)
        send(0, c, s0, ra)

    pin_row = to_row(pin_hi) * 256.0 + to_row(pin_lo)
    walk_row = to_row(walk_tab)
    match = iota((PINS, SLOTS), 0).astype(F32) == pin_row
    weights = jnp.where(match, walk_row, 0.0)
    pin_w[...] = weights.astype(BF)
    pdeg[...] = jnp.maximum(jnp.sum(weights, axis=1, keepdims=True), 1.0)
    own_walk = to_column(walk_tab)
    degree_row = jnp.sum(pin_t[...].astype(F32) * own_walk, axis=0, keepdims=True)
    slot_degree = jnp.sum(pin_t[...].astype(F32) * degree_row, axis=1, keepdims=True)
    scale_col[...] = own_walk / jnp.maximum(slot_degree, 1.0)
    feat_t[...] = feat[...].T

    pltpu.make_async_copy(idx_r, idx_r, idx_sem.at[1]).wait()
    sent_idx = idx_s.at[pl.ds(0, DEV - 1)]
    pltpu.make_async_copy(sent_idx, sent_idx, idx_sem.at[0]).wait()

    @pl.loop(0, DEV)
    def _(row):
        table[pl.ds(row, 1), :] = idx_r[row].astype(F32)

    received = table[...].astype(jnp.int32)
    brd_tab = (received % 256).astype(F32)
    bwalk_tab = (received // 256).astype(F32)
    brd_t[...] = (iota((SLOTS, BOARDS), 1).astype(F32) == to_column(brd_tab)).astype(F32).astype(BF)
    walk_col[...] = to_column(bwalk_tab)
    match = iota((BOARDS, SLOTS), 0).astype(F32) == to_row(brd_tab)
    weights = jnp.where(match, to_row(bwalk_tab), 0.0)
    brd_w[...] = weights.astype(BF)
    bdeg[...] = jnp.maximum(jnp.sum(weights, axis=1, keepdims=True), 1.0)

    @pl.loop(0, C)
    def _(c):
        wait_received(0, c, ra)
        brow_buf[0] = (mm(brd_w[...], ra[c]) / bdeg[...]).astype(BF)

        @pl.loop(0, SLOTS // TILE)
        def _(i):
            s1[c, tile(i)] = mm(brd_t[tile(i), :], brow_buf[0]).astype(BF)

        send(1, c, s1, rb)

    brd_w[...] = (brd_w[...].astype(F32) > 0.0).astype(F32).astype(BF)
    loads[2].wait()
    loads[3].wait()
    upd[...] = jnp.zeros_like(upd)

    @pl.loop(0, C)
    def _(c):
        wait_received(1, c, rb)
        part = (mm(pin_w[...], rb[c]) / pdeg[...]).astype(BF)
        small[...] = part
        nb_t[cols(c), :] = part.T

        @pl.loop(0, C)
        def _(n):
            upd[:, cols(n)] += mm(small[...], wu[cols(c), cols(n)])

    @pl.loop(0, C)
    def _(n):
        feat[:, cols(n)] = (cot[:, cols(n)].astype(F32) * silu_slope(upd[:, cols(n)])).astype(BF)

    @pl.loop(0, C)
    def _(c):
        wait_sent(0, c, s0)
        small[...] = mm(feat[:, :H], wu[cols(c), :], ((1,), (1,))).astype(BF)

        @pl.loop(0, SLOTS // TILE)
        def _(i):
            s0[c, tile(i)] = (scale_col[tile(i), :] * mm(pin_t[tile(i), :], small[...])).astype(BF)

        send(2, c, s0, ra)

    @pl.loop(0, C)
    def _(n):
        wu[cols(n), :] = mm(nb_t[cols(n), :], feat[:, :H]).astype(BF)

    update_steps = [
        grad_steps(wu, gu, 0, i, grad_buf.at[i // 2], (i % 2) * 1024, axis, gsend_sem.at[i], grecv_sem.at[i])
        for i, axis in enumerate((2, 0, 2, 1))
    ]
    for steps in update_steps:
        steps[0]()

    @pl.loop(0, C)
    def _(n):
        update = upd[:, cols(n)]
        out[:, cols(n)] = (hid[:, cols(n)].astype(F32) + update * jax.nn.sigmoid(update)).astype(BF)

    pin_w[...] = (pin_w[...].astype(F32) > 0.0).astype(F32).astype(BF)

    for c in range(C):
        wait_received(2, c, ra)
        wait_sent(1, c, s1)
        board_grad = mm(brd_w[...], ra[c]) / bdeg[...]
        high = board_grad.astype(BF)
        brow_buf[0] = high
        brow_buf[1] = (board_grad - high.astype(F32)).astype(BF)

        @pl.loop(0, SLOTS // TILE)
        def _(i):
            pick = brd_t[tile(i), :]
            rows = mm(pick, brow_buf[0]) + mm(pick, brow_buf[1])
            s1[c, tile(i)] = (walk_col[tile(i), :] * rows).astype(BF)

        send(3, c, s1, rb)

    message_steps = []
    for c in range(C):
        wait_received(3, c, rb)
        grad = cot[:, cols(c)].astype(F32) + mm(pin_w[...], rb[c])
        small[...] = (grad * silu_slope(pre[:, cols(c)])).astype(BF)

        @pl.loop(0, F // TILE)
        def _(i):
            wm[tile(i), cols(c)] = mm(feat_t[tile(i), :], small[...]).astype(BF)

        message_steps.append([
            grad_steps(
                wm, gm, h * 1024, c, ra.at[c], h * 1024, (2 * c + h) % 3,
                gsend_sem.at[4 + 2 * c + h], grecv_sem.at[4 + 2 * c + h],
            )
            for h in range(2)
        ])
        for steps in update_steps:
            steps[1 + c]()
        for back in range(c + 1):
            for steps in message_steps[c - back]:
                steps[back]()

    for tick in range(1, 7):
        if tick < 3:
            for steps in update_steps:
                steps[4 + tick]()
        for back in range(tick, min(tick + C, 7)):
            for steps in message_steps[C - 1 + tick - back]:
                steps[back]()

    @pl.loop(0, C)
    def _(c):
        wait_sent(2, c, s0)
        wait_sent(3, c, s1)

    for steps in update_steps + message_steps[0] + message_steps[1] + message_steps[2] + message_steps[3]:
        steps[7]()


def body(features, w_message, w_update, cotangent, slot_pin, slot_board, slot_walk, pair_count):
    hbm = pl.BlockSpec(memory_space=pl.ANY)
    vmem = pl.BlockSpec(memory_space=pltpu.VMEM)
    sem = pltpu.SemaphoreType.DMA
    output, gm, gu = pl.pallas_call(
        main_kernel,
        out_shape=(
            pltpu.VMEM((PINS, H), BF),
            pltpu.VMEM((F, H), BF),
            pltpu.VMEM((H, H), BF),
        ),
        in_specs=[hbm] * 4 + [vmem] * 4,
        out_specs=(vmem, vmem, vmem),
        scratch_shapes=[
            pltpu.VMEM((PINS, F), BF), pltpu.VMEM((F, H), BF), pltpu.VMEM((H, H), BF), pltpu.VMEM((PINS, H), BF),
            pltpu.VMEM((PINS, H), F32), pltpu.VMEM((PINS, H), BF),
            pltpu.VMEM((C, SLOTS, W), BF), pltpu.VMEM((C, SLOTS, W), BF),
            pltpu.VMEM((C, SLOTS, W), BF), pltpu.VMEM((C, SLOTS, W), BF),
            pltpu.VMEM((SLOTS, PINS), BF), pltpu.VMEM((PINS, SLOTS), BF),
            pltpu.VMEM((SLOTS, BOARDS), BF), pltpu.VMEM((BOARDS, SLOTS), BF),
            pltpu.VMEM((F, PINS), BF),
            pltpu.VMEM((PINS, H), F32), pltpu.VMEM((H, PINS), BF),
            pltpu.VMEM((SLOTS, 1), F32), pltpu.VMEM((SLOTS, 1), F32), pltpu.VMEM((PINS, 1), F32), pltpu.VMEM((BOARDS, 1), F32),
            pltpu.VMEM((2, BOARDS, W), BF), pltpu.VMEM((2, SLOTS, W), BF), pltpu.VMEM((PINS, W), BF),
            pltpu.VMEM((DEV, DEV), F32), pltpu.VMEM((DEV, 1, DEV), jnp.int32), pltpu.VMEM((DEV, 1, DEV), jnp.int32),
            sem((4,)), sem((2,)), sem((4, C)), sem((4, C)), sem((12, 6)), sem((12, 6)),
        ],
        name="layer",
        compiler_params=pltpu.CompilerParams(
            collective_id=0, has_side_effects=True, vmem_limit_bytes=54 * 1024 * 1024
        ),
    )(
        features, w_message, w_update, cotangent,
        slot_pin[0].T, slot_board[0].T, slot_walk[0].T, pair_count,
    )
    return output, gm, gu


def solution(mesh):
    in_specs = (
        P(("pin", "board"), None),
        P(),
        P(),
        P(("pin", "board"), None),
        P(("pin", "board"), None, None),
        P(("pin", "board"), None, None),
        P(("pin", "board"), None, None),
        P(("pin", "board"), None),
    )
    out_specs = (P(("pin", "board"), None), P(), P())
    return jax.shard_map(body, mesh=mesh, in_specs=in_specs, out_specs=out_specs, check_vma=False)
```

```python
import jax
import jax.numpy as jnp
from jax import lax
from jax.experimental import pallas as pl
from jax.experimental.pallas import tpu as pltpu
from jax.sharding import PartitionSpec as P

MESH = pl.DeviceIdType.MESH
BF = jnp.bfloat16
F32 = jnp.float32
DEV = 128
CAP = 16
SLOTS = DEV * CAP
PINS = 512
BOARDS = 256
F = 2048
H = 1024
W = 256
C = H // W
TILE = 512

PLAN = (
    (
        (1, 0),
    ),
    (
        (2, 0), (0, 1),
    ),
    (
        (3, 0), (1, 1),
    ),
    (
        (4, 0), (2, 1), (3, 1), (4, 1), (0, 2), (1, 2), (2, 2), (3, 2),
        (4, 2), (0, 3), (1, 3), (2, 3), (3, 3), (4, 3), (0, 4), (1, 4),
        (2, 4), (3, 4), (4, 4), (0, 5), (1, 5), (2, 5), (3, 5), (4, 5),
        (0, 6), (1, 6), (2, 6), (3, 6), (4, 6),
    ),
)


def silu_slope(value):
    sig = jax.nn.sigmoid(value)
    return sig * (1.0 + value * (1.0 - sig))


def mm(a, b, dims=((1,), (0,))):
    return lax.dot_general(a, b, (dims, ((), ())), preferred_element_type=F32)


def iota(shape, axis):
    return lax.broadcasted_iota(jnp.int32, shape, axis)


def places():
    pin = lax.axis_index("pin")
    z, x, y = lax.div(pin, 8), lax.rem(lax.div(pin, 2), 4), lax.axis_index("board")
    zs = [lax.rem(z + i, 4) * 8 for i in range(4)]
    xs = [lax.rem(x + i, 4) * 2 for i in range(4)]
    ys = [lax.rem(y + i, 4) for i in range(4)]
    return zs, xs, lax.rem(pin, 2), ys


def for_peers(visit):
    zs, xs, core, ys = places()

    def group(step, first):
        dc, dy = lax.div(step, 4), lax.rem(step, 4)
        c = lax.rem(core + dc, 2)
        rows = [lax.rem(ys[i] + dy, 4) for i in range(4)]
        for i in range(4):
            for dz in range(4):
                if first and i == 0 and dz == 0:
                    continue
                dx = (i + dz) % 4
                visit((zs[dz] + xs[dx] + c, rows[(dx + dz) % 4]))

    group(jnp.int32(0), True)

    @pl.loop(1, 8)
    def _(step):
        group(step, False)


def line_of(axis):
    zs, xs, core, ys = places()
    tables, scale = [zs, xs, ys], (8, 2, 1)[axis]
    others = []
    for i in (1, 3, 2):
        place = [zs[0], xs[0], ys[0]]
        place[axis] = tables[axis][i]
        others.append(((place[0] + place[1] + core, place[2]), lax.div(place[axis], scale), i - 1))
    return lax.div(tables[axis][0], scale), others


def plane_of(axis):
    zs, xs, core, ys = places()
    tables, scales = [zs, xs, ys], (8, 2, 1)
    b, d = (axis + 1) % 3, (axis + 2) % 3
    rb = [lax.div(v, scales[b]) * 4 for v in tables[b]]
    rd = [lax.div(v, scales[d]) for v in tables[d]]
    others = []
    for i in range(4):
        for j in range(4):
            if i or j:
                k, m = i, (i + j) % 4
                if not (k or m):
                    continue
                place = [zs[0], xs[0], ys[0]]
                place[b], place[d] = tables[b][k], tables[d][m]
                others.append(((place[0] + place[1] + core, place[2]), rb[k] + rd[m], 4 * k + m - 1))
    return rb[0] + rd[0], others


def grad_steps(src, dst, row0, c, buf, brow0, axis, send_sem, recv_sem):
    pin = lax.axis_index("pin")
    core = lax.rem(pin, 2)
    partner = (pin + 1 - 2 * core, lax.axis_index("board"))
    quarter, line = line_of(axis)
    rank, plane = plane_of(axis)
    half = W // 2
    own = pl.ds(pl.multiple_of(c * W + core * half, half), half)
    other = pl.ds(pl.multiple_of(c * W + (1 - core) * half, half), half)
    left, right = pl.ds(0, half), pl.ds(half, half)
    every = pl.ds(row0, 1024)
    pair_buf = buf.at[pl.ds(brow0, 1024), left]
    line_buf = buf.at[pl.ds(brow0, 768), right]
    plane_buf = buf.at[pl.ds(brow0 + 768, 240), right]

    def line_rows(q):
        return pl.ds(pl.multiple_of(row0 + q * 256, 256), 256)

    def plane_rows(r):
        return pl.ds(pl.multiple_of(row0 + quarter * 256 + r * 16, 16), 16)

    def put(a, b, step, device):
        pltpu.make_async_remote_copy(
            a, b, send_sem.at[step], recv_sem.at[step], device_id=device, device_id_type=MESH
        ).start()

    def arrived(like, step):
        pltpu.make_async_copy(like, like, recv_sem.at[step]).wait()

    def pair_out():
        put(src.at[every, other], pair_buf, 0, partner)

    def line_out():
        arrived(pair_buf, 0)
        src[every, own] = (src[every, own].astype(F32) + pair_buf[...].astype(F32)).astype(BF)
        for device, q, slot in line:
            put(src.at[line_rows(q), own], buf.at[pl.ds(brow0 + slot * 256, 256), right], 1, device)

    def plane_out():
        arrived(line_buf, 1)
        total = src[line_rows(quarter), own].astype(F32)
        for i in range(3):
            total += buf[brow0 + i * 256:brow0 + (i + 1) * 256, half:].astype(F32)
        src[line_rows(quarter), own] = total.astype(BF)

        for device, r, slot in plane:
            put(src.at[plane_rows(r), own], buf.at[pl.ds(brow0 + 768 + slot * 16, 16), right], 2, device)

    def plane_back():
        arrived(plane_buf, 2)
        parts = plane_buf[...].astype(F32).reshape(15, 16, half)
        total = src[plane_rows(rank), own].astype(F32) + jnp.sum(parts, axis=0)
        dst[plane_rows(rank), own] = total.astype(BF)

        piece = dst.at[plane_rows(rank), own]
        for device, _, _ in plane:
            put(piece, piece, 3, device)

    def line_back():
        arrived(plane_buf, 3)
        piece = dst.at[line_rows(quarter), own]
        for device, _, _ in line:
            put(piece, piece, 4, device)

    def pair_back():
        arrived(line_buf, 4)
        piece = dst.at[every, own]
        put(piece, piece, 5, partner)

    def finish():
        arrived(pair_buf, 5)

    def sent():
        for step, like in enumerate((pair_buf, line_buf, plane_buf, plane_buf, line_buf, pair_buf)):
            pltpu.make_async_copy(like, like, send_sem.at[step]).wait()

    return [pair_out, line_out, plane_out, plane_back, line_back, pair_back, finish, sent]


def to_column(table):
    pick = (iota((SLOTS, DEV), 0) // CAP == iota((SLOTS, DEV), 1)).astype(F32).astype(BF)
    rows = mm(pick, table.astype(BF))
    keep = iota((SLOTS, DEV), 0) % CAP == iota((SLOTS, DEV), 1)
    return jnp.sum(jnp.where(keep, rows, 0.0), axis=1, keepdims=True)


def to_row(table):
    pick = (iota((DEV, SLOTS), 1) % CAP == iota((DEV, SLOTS), 0)).astype(F32).astype(BF)
    columns = mm(table.astype(BF), pick)
    keep = iota((DEV, SLOTS), 1) // CAP == iota((DEV, SLOTS), 0)
    return jnp.sum(jnp.where(keep, columns, 0.0), axis=0, keepdims=True)


def main_kernel(
    feat_hbm, wm_hbm, wu_hbm, cot_hbm, spin_ref, sboard_ref, swalk_ref, count_ref,
    out, gm, gu,
    feat, wm, wu, cot,
    pre, hid, s0, s1, ra, rb,
    pin_t, pin_w, brd_t, brd_w, feat_t,
    upd, nb_t, scale_col, walk_col, pdeg, bdeg, brow_buf, grad_buf, small,
    table, idx_s, idx_r,
    load_sem, idx_sem, send_sem, recv_sem, gsend_sem, grecv_sem,
):
    me = lax.axis_index("pin") * 4 + lax.axis_index("board")
    barrier = pltpu.get_barrier_semaphore()

    loads = [
        pltpu.make_async_copy(feat_hbm, feat, load_sem.at[0]),
        pltpu.make_async_copy(wm_hbm, wm, load_sem.at[1]),
        pltpu.make_async_copy(wu_hbm, wu, load_sem.at[2]),
        pltpu.make_async_copy(cot_hbm, cot, load_sem.at[3]),
    ]
    for load in loads:
        load.start()

    for_peers(lambda peer: pl.semaphore_signal(barrier, inc=1, device_id=peer, device_id_type=MESH))

    def block(device):
        return pl.ds(pl.multiple_of(device * CAP, CAP), CAP)

    def send(phase, c, src, dst):
        pltpu.make_async_copy(src.at[c, block(me)], dst.at[c, block(me)], recv_sem.at[phase, c]).start()

        def put(peer):
            pltpu.make_async_remote_copy(
                src.at[c, block(peer[0] * 4 + peer[1])], dst.at[c, block(me)],
                send_sem.at[phase, c], recv_sem.at[phase, c],
                device_id=peer, device_id_type=MESH,
            ).start()

        for_peers(put)

    def wait_sent(phase, c, src):
        part = src.at[c, pl.ds(0, (DEV - 1) * CAP)]
        pltpu.make_async_copy(part, part, send_sem.at[phase, c]).wait()

    def wait_received(phase, c, dst):
        pltpu.make_async_copy(dst.at[c], dst.at[c], recv_sem.at[phase, c]).wait()

    def cols(c):
        return pl.ds(pl.multiple_of(c * W, W), W)

    def tile(i):
        return pl.ds(pl.multiple_of(i * TILE, TILE), TILE)

    live = iota((CAP, DEV), 0) < count_ref[...]
    walks = jnp.where(live, swalk_ref[...], 0)
    table[...] = jnp.zeros_like(table)
    table[:CAP, :] = (walks * 512 + spin_ref[...]).astype(F32)
    packed = table[...].T.astype(jnp.int32)
    pin_hi = ((packed // 256) % 2).astype(F32)
    pin_lo = (packed % 256).astype(F32)
    walk_tab = (packed // 512).astype(F32)
    pin_col = to_column(pin_hi) * 256.0 + to_column(pin_lo)
    pin_t[...] = (iota((SLOTS, PINS), 1).astype(F32) == pin_col).astype(F32).astype(BF)
    loads[0].wait()
    loads[1].wait()

    def project(c):
        value = mm(feat[...], wm[:, cols(c)])
        pre[:, cols(c)] = value
        hid[:, cols(c)] = (value * jax.nn.sigmoid(value)).astype(BF)

        @pl.loop(0, SLOTS // TILE)
        def _(i):
            s0[c, tile(i)] = mm(pin_t[tile(i), :], hid[:, cols(c)]).astype(BF)

    project(0)
    pl.semaphore_wait(barrier, DEV - 1)
    send(0, 0, s0, ra)

    table[:CAP, :] = (walks * 256 + sboard_ref[...]).astype(F32)
    table[...] = table[...].T

    @pl.loop(0, DEV)
    def _(row):
        idx_s[row] = table[pl.ds(row, 1), :].astype(jnp.int32)

    pltpu.make_async_copy(idx_s.at[me], idx_r.at[me], idx_sem.at[1]).start()

    def put_table(peer):
        pltpu.make_async_remote_copy(
            idx_s.at[peer[0] * 4 + peer[1]], idx_r.at[me], idx_sem.at[0], idx_sem.at[1],
            device_id=peer, device_id_type=MESH,
        ).start()

    for_peers(put_table)

    @pl.loop(1, C)
    def _(c):
        project(c)
        send(0, c, s0, ra)

    pin_row = to_row(pin_hi) * 256.0 + to_row(pin_lo)
    walk_row = to_row(walk_tab)
    match = iota((PINS, SLOTS), 0).astype(F32) == pin_row
    weights = jnp.where(match, walk_row, 0.0)
    pin_w[...] = weights.astype(BF)
    pdeg[...] = jnp.maximum(jnp.sum(weights, axis=1, keepdims=True), 1.0)
    own_walk = to_column(walk_tab)
    degree_row = jnp.sum(pin_t[...].astype(F32) * own_walk, axis=0, keepdims=True)
    slot_degree = jnp.sum(pin_t[...].astype(F32) * degree_row, axis=1, keepdims=True)
    scale_col[...] = own_walk / jnp.maximum(slot_degree, 1.0)
    feat_t[...] = feat[...].T

    pltpu.make_async_copy(idx_r, idx_r, idx_sem.at[1]).wait()
    sent_idx = idx_s.at[pl.ds(0, DEV - 1)]
    pltpu.make_async_copy(sent_idx, sent_idx, idx_sem.at[0]).wait()

    @pl.loop(0, DEV)
    def _(row):
        table[pl.ds(row, 1), :] = idx_r[row].astype(F32)

    received = table[...].astype(jnp.int32)
    brd_tab = (received % 256).astype(F32)
    bwalk_tab = (received // 256).astype(F32)
    brd_t[...] = (iota((SLOTS, BOARDS), 1).astype(F32) == to_column(brd_tab)).astype(F32).astype(BF)
    walk_col[...] = to_column(bwalk_tab)
    match = iota((BOARDS, SLOTS), 0).astype(F32) == to_row(brd_tab)
    weights = jnp.where(match, to_row(bwalk_tab), 0.0)
    brd_w[...] = weights.astype(BF)
    bdeg[...] = jnp.maximum(jnp.sum(weights, axis=1, keepdims=True), 1.0)

    @pl.loop(0, C)
    def _(c):
        wait_received(0, c, ra)
        brow_buf[0] = (mm(brd_w[...], ra[c]) / bdeg[...]).astype(BF)

        @pl.loop(0, SLOTS // TILE)
        def _(i):
            s1[c, tile(i)] = mm(brd_t[tile(i), :], brow_buf[0]).astype(BF)

        send(1, c, s1, rb)

    brd_w[...] = (brd_w[...].astype(F32) > 0.0).astype(F32).astype(BF)
    loads[2].wait()
    loads[3].wait()
    upd[...] = jnp.zeros_like(upd)

    @pl.loop(0, C)
    def _(c):
        wait_received(1, c, rb)
        part = (mm(pin_w[...], rb[c]) / pdeg[...]).astype(BF)
        small[...] = part
        nb_t[cols(c), :] = part.T

        @pl.loop(0, C)
        def _(n):
            upd[:, cols(n)] += mm(small[...], wu[cols(c), cols(n)])

    @pl.loop(0, C)
    def _(n):
        feat[:, cols(n)] = (cot[:, cols(n)].astype(F32) * silu_slope(upd[:, cols(n)])).astype(BF)

    @pl.loop(0, C)
    def _(c):
        wait_sent(0, c, s0)
        small[...] = mm(feat[:, :H], wu[cols(c), :], ((1,), (1,))).astype(BF)

        @pl.loop(0, SLOTS // TILE)
        def _(i):
            s0[c, tile(i)] = (scale_col[tile(i), :] * mm(pin_t[tile(i), :], small[...])).astype(BF)

        send(2, c, s0, ra)

    @pl.loop(0, C)
    def _(n):
        wu[cols(n), :] = mm(nb_t[cols(n), :], feat[:, :H]).astype(BF)

    update_steps = [
        grad_steps(wu, gu, 0, i, grad_buf.at[i // 2], (i % 2) * 1024, axis, gsend_sem.at[i], grecv_sem.at[i])
        for i, axis in enumerate((2, 0, 2, 1))
    ]
    for steps in update_steps:
        steps[0]()

    @pl.loop(0, C)
    def _(n):
        update = upd[:, cols(n)]
        out[:, cols(n)] = (hid[:, cols(n)].astype(F32) + update * jax.nn.sigmoid(update)).astype(BF)

    pin_w[...] = (pin_w[...].astype(F32) > 0.0).astype(F32).astype(BF)

    for c in range(C):
        wait_received(2, c, ra)
        wait_sent(1, c, s1)
        board_grad = mm(brd_w[...], ra[c]) / bdeg[...]
        high = board_grad.astype(BF)
        brow_buf[0] = high
        brow_buf[1] = (board_grad - high.astype(F32)).astype(BF)

        @pl.loop(0, SLOTS // TILE)
        def _(i):
            pick = brd_t[tile(i), :]
            rows = mm(pick, brow_buf[0]) + mm(pick, brow_buf[1])
            s1[c, tile(i)] = (walk_col[tile(i), :] * rows).astype(BF)

        send(3, c, s1, rb)

    message_steps = []
    for c in range(C):
        wait_received(3, c, rb)
        grad = cot[:, cols(c)].astype(F32) + mm(pin_w[...], rb[c])
        small[...] = (grad * silu_slope(pre[:, cols(c)])).astype(BF)

        @pl.loop(0, F // TILE)
        def _(i):
            wm[tile(i), cols(c)] = mm(feat_t[tile(i), :], small[...]).astype(BF)

        message_steps.append([
            grad_steps(
                wm, gm, h * 1024, c, ra.at[c], h * 1024, (2 * c + h) % 3,
                gsend_sem.at[4 + 2 * c + h], grecv_sem.at[4 + 2 * c + h],
            )
            for h in range(2)
        ])
        blocks = [update_steps] + message_steps
        for block_set, step in PLAN[c]:
            for steps in blocks[block_set]:
                steps[step]()

    @pl.loop(0, C)
    def _(c):
        wait_sent(2, c, s0)
        wait_sent(3, c, s1)

    for steps in update_steps + message_steps[0] + message_steps[1] + message_steps[2] + message_steps[3]:
        steps[7]()


def body(features, w_message, w_update, cotangent, slot_pin, slot_board, slot_walk, pair_count):
    hbm = pl.BlockSpec(memory_space=pl.ANY)
    vmem = pl.BlockSpec(memory_space=pltpu.VMEM)
    sem = pltpu.SemaphoreType.DMA
    output, gm, gu = pl.pallas_call(
        main_kernel,
        out_shape=(
            pltpu.VMEM((PINS, H), BF),
            pltpu.VMEM((F, H), BF),
            pltpu.VMEM((H, H), BF),
        ),
        in_specs=[hbm] * 4 + [vmem] * 4,
        out_specs=(vmem, vmem, vmem),
        scratch_shapes=[
            pltpu.VMEM((PINS, F), BF), pltpu.VMEM((F, H), BF), pltpu.VMEM((H, H), BF), pltpu.VMEM((PINS, H), BF),
            pltpu.VMEM((PINS, H), F32), pltpu.VMEM((PINS, H), BF),
            pltpu.VMEM((C, SLOTS, W), BF), pltpu.VMEM((C, SLOTS, W), BF),
            pltpu.VMEM((C, SLOTS, W), BF), pltpu.VMEM((C, SLOTS, W), BF),
            pltpu.VMEM((SLOTS, PINS), BF), pltpu.VMEM((PINS, SLOTS), BF),
            pltpu.VMEM((SLOTS, BOARDS), BF), pltpu.VMEM((BOARDS, SLOTS), BF),
            pltpu.VMEM((F, PINS), BF),
            pltpu.VMEM((PINS, H), F32), pltpu.VMEM((H, PINS), BF),
            pltpu.VMEM((SLOTS, 1), F32), pltpu.VMEM((SLOTS, 1), F32), pltpu.VMEM((PINS, 1), F32), pltpu.VMEM((BOARDS, 1), F32),
            pltpu.VMEM((2, BOARDS, W), BF), pltpu.VMEM((2, SLOTS, W), BF), pltpu.VMEM((PINS, W), BF),
            pltpu.VMEM((DEV, DEV), F32), pltpu.VMEM((DEV, 1, DEV), jnp.int32), pltpu.VMEM((DEV, 1, DEV), jnp.int32),
            sem((4,)), sem((2,)), sem((4, C)), sem((4, C)), sem((12, 6)), sem((12, 6)),
        ],
        name="layer",
        compiler_params=pltpu.CompilerParams(
            collective_id=0, has_side_effects=True, vmem_limit_bytes=54 * 1024 * 1024
        ),
    )(
        features, w_message, w_update, cotangent,
        slot_pin[0].T, slot_board[0].T, slot_walk[0].T, pair_count,
    )
    return output, gm, gu


def solution(mesh):
    in_specs = (
        P(("pin", "board"), None),
        P(),
        P(),
        P(("pin", "board"), None),
        P(("pin", "board"), None, None),
        P(("pin", "board"), None, None),
        P(("pin", "board"), None, None),
        P(("pin", "board"), None),
    )
    out_specs = (P(("pin", "board"), None), P(), P())
    return jax.shard_map(body, mesh=mesh, in_specs=in_specs, out_specs=out_specs, check_vma=False)
```

```python
import jax
import jax.numpy as jnp
from jax import lax
from jax.experimental import pallas as pl
from jax.experimental.pallas import tpu as pltpu
from jax.sharding import PartitionSpec as P

MESH = pl.DeviceIdType.MESH
BF = jnp.bfloat16
F32 = jnp.float32
DEV = 128
CAP = 16
SLOTS = DEV * CAP
PINS = 512
BOARDS = 256
F = 2048
H = 1024
W = 256
C = H // W
TILE = 512

PLAN = (
    (
        (1, 0),
    ),
    (
        (2, 0), (0, 1),
    ),
    (
        (3, 0), (1, 1),
    ),
    (
        (4, 0), (2, 1), (3, 1), (4, 1), (0, 2), (1, 2), (2, 2), (3, 2),
        (4, 2), (0, 3), (1, 3), (2, 3), (3, 3), (4, 3), (0, 4), (1, 4),
        (2, 4), (3, 4), (4, 4), (0, 5), (1, 5), (2, 5), (3, 5), (4, 5),
        (0, 6), (1, 6), (2, 6), (3, 6), (4, 6),
    ),
)


def silu_slope(value):
    sig = jax.nn.sigmoid(value)
    return sig * (1.0 + value * (1.0 - sig))


def mm(a, b, dims=((1,), (0,))):
    return lax.dot_general(a, b, (dims, ((), ())), preferred_element_type=F32)


def iota(shape, axis):
    return lax.broadcasted_iota(jnp.int32, shape, axis)


def places():
    pin = lax.axis_index("pin")
    z, x, y = lax.div(pin, 8), lax.rem(lax.div(pin, 2), 4), lax.axis_index("board")
    zs = [lax.rem(z + i, 4) * 8 for i in range(4)]
    xs = [lax.rem(x + i, 4) * 2 for i in range(4)]
    ys = [lax.rem(y + i, 4) for i in range(4)]
    return zs, xs, lax.rem(pin, 2), ys


def for_peers(visit):
    zs, xs, core, ys = places()

    def group(step, first):
        dc, dy = lax.div(step, 4), lax.rem(step, 4)
        c = lax.rem(core + dc, 2)
        rows = [lax.rem(ys[i] + dy, 4) for i in range(4)]
        for i in range(4):
            for dz in range(4):
                if first and i == 0 and dz == 0:
                    continue
                dx = (i + dz) % 4
                visit((zs[dz] + xs[dx] + c, rows[(dx + dz) % 4]))

    group(jnp.int32(0), True)

    @pl.loop(1, 8)
    def _(step):
        group(step, False)


def line_of(axis):
    zs, xs, core, ys = places()
    tables, scale = [zs, xs, ys], (8, 2, 1)[axis]
    others = []
    for i in (1, 3, 2):
        place = [zs[0], xs[0], ys[0]]
        place[axis] = tables[axis][i]
        others.append(((place[0] + place[1] + core, place[2]), lax.div(place[axis], scale), i - 1))
    return lax.div(tables[axis][0], scale), others


def plane_of(axis):
    zs, xs, core, ys = places()
    tables, scales = [zs, xs, ys], (8, 2, 1)
    b, d = (axis + 1) % 3, (axis + 2) % 3
    rb = [lax.div(v, scales[b]) * 4 for v in tables[b]]
    rd = [lax.div(v, scales[d]) for v in tables[d]]
    others = []
    for i in range(4):
        for j in range(4):
            if i or j:
                k, m = i, (i + j) % 4
                if not (k or m):
                    continue
                place = [zs[0], xs[0], ys[0]]
                place[b], place[d] = tables[b][k], tables[d][m]
                others.append(((place[0] + place[1] + core, place[2]), rb[k] + rd[m], 4 * k + m - 1))
    return rb[0] + rd[0], others


def grad_steps(src, dst, row0, c, buf, brow0, axis, send_sem, recv_sem):
    pin = lax.axis_index("pin")
    core = lax.rem(pin, 2)
    partner = (pin + 1 - 2 * core, lax.axis_index("board"))
    quarter, line = line_of(axis)
    rank, plane = plane_of(axis)
    half = W // 2
    own = pl.ds(pl.multiple_of(c * W + core * half, half), half)
    other = pl.ds(pl.multiple_of(c * W + (1 - core) * half, half), half)
    left, right = pl.ds(0, half), pl.ds(half, half)
    every = pl.ds(row0, 1024)
    pair_buf = buf.at[pl.ds(brow0, 1024), left]
    line_buf = buf.at[pl.ds(brow0, 768), right]
    plane_buf = buf.at[pl.ds(brow0 + 768, 240), right]

    def line_rows(q):
        return pl.ds(pl.multiple_of(row0 + q * 256, 256), 256)

    def plane_rows(r):
        return pl.ds(pl.multiple_of(row0 + quarter * 256 + r * 16, 16), 16)

    def put(a, b, step, device):
        pltpu.make_async_remote_copy(
            a, b, send_sem.at[step], recv_sem.at[step], device_id=device, device_id_type=MESH
        ).start()

    def arrived(like, step):
        pltpu.make_async_copy(like, like, recv_sem.at[step]).wait()

    def pair_out():
        put(src.at[every, other], pair_buf, 0, partner)

    def line_out():
        arrived(pair_buf, 0)
        src[every, own] = (src[every, own].astype(F32) + pair_buf[...].astype(F32)).astype(BF)
        for device, q, slot in line:
            put(src.at[line_rows(q), own], buf.at[pl.ds(brow0 + slot * 256, 256), right], 1, device)

    def plane_out():
        arrived(line_buf, 1)
        total = src[line_rows(quarter), own].astype(F32)
        for i in range(3):
            total += buf[brow0 + i * 256:brow0 + (i + 1) * 256, half:].astype(F32)
        src[line_rows(quarter), own] = total.astype(BF)

        for device, r, slot in plane:
            put(src.at[plane_rows(r), own], buf.at[pl.ds(brow0 + 768 + slot * 16, 16), right], 2, device)

    def plane_back():
        arrived(plane_buf, 2)
        parts = plane_buf[...].astype(F32).reshape(15, 16, half)
        total = src[plane_rows(rank), own].astype(F32) + jnp.sum(parts, axis=0)
        dst[plane_rows(rank), own] = total.astype(BF)

        piece = dst.at[plane_rows(rank), own]
        for device, _, _ in plane:
            put(piece, piece, 3, device)

    def line_back():
        arrived(plane_buf, 3)
        piece = dst.at[line_rows(quarter), own]
        for device, _, _ in line:
            put(piece, piece, 4, device)

    def pair_back():
        arrived(line_buf, 4)
        piece = dst.at[every, own]
        put(piece, piece, 5, partner)

    def finish():
        arrived(pair_buf, 5)

    def sent():
        for step, like in enumerate((pair_buf, line_buf, plane_buf, plane_buf, line_buf, pair_buf)):
            pltpu.make_async_copy(like, like, send_sem.at[step]).wait()

    return [pair_out, line_out, plane_out, plane_back, line_back, pair_back, finish, sent]


def to_column(table):
    pick = (iota((SLOTS, DEV), 0) // CAP == iota((SLOTS, DEV), 1)).astype(F32).astype(BF)
    rows = mm(pick, table.astype(BF))
    keep = iota((SLOTS, DEV), 0) % CAP == iota((SLOTS, DEV), 1)
    return jnp.sum(jnp.where(keep, rows, 0.0), axis=1, keepdims=True)


def to_row(table):
    pick = (iota((DEV, SLOTS), 1) % CAP == iota((DEV, SLOTS), 0)).astype(F32).astype(BF)
    columns = mm(table.astype(BF), pick)
    keep = iota((DEV, SLOTS), 1) // CAP == iota((DEV, SLOTS), 0)
    return jnp.sum(jnp.where(keep, columns, 0.0), axis=0, keepdims=True)


def main_kernel(
    feat_hbm, wm_hbm, wu_hbm, cot_hbm, spin_ref, sboard_ref, swalk_ref, count_ref,
    out, gm, gu,
    feat, wm, wu, cot,
    pre, hid, s0, s1, ra, rb,
    pin_t, pin_w, brd_t, brd_w, feat_t,
    upd, nb_t, scale_col, walk_col, pdeg, bdeg, brow_buf, grad_buf, small,
    table, idx_s, idx_r,
    load_sem, idx_sem, send_sem, recv_sem, gsend_sem, grecv_sem,
):
    me = lax.axis_index("pin") * 4 + lax.axis_index("board")
    barrier = pltpu.get_barrier_semaphore()

    loads = [
        pltpu.make_async_copy(feat_hbm, feat, load_sem.at[0]),
        pltpu.make_async_copy(wm_hbm, wm, load_sem.at[1]),
        pltpu.make_async_copy(wu_hbm, wu, load_sem.at[2]),
        pltpu.make_async_copy(cot_hbm, cot, load_sem.at[3]),
    ]
    for load in loads:
        load.start()

    zs, xs, core, ys = places()
    for i in range(1, DEV):
        peer = (zs[i // 32] + xs[i // 8 % 4] + (core if i % 8 < 4 else 1 - core), ys[i % 4])
        pl.semaphore_signal(barrier, inc=1, device_id=peer, device_id_type=MESH)

    def block(device):
        return pl.ds(pl.multiple_of(device * CAP, CAP), CAP)

    def send(phase, c, src, dst):
        pltpu.make_async_copy(src.at[c, block(me)], dst.at[c, block(me)], recv_sem.at[phase, c]).start()

        def put(peer):
            pltpu.make_async_remote_copy(
                src.at[c, block(peer[0] * 4 + peer[1])], dst.at[c, block(me)],
                send_sem.at[phase, c], recv_sem.at[phase, c],
                device_id=peer, device_id_type=MESH,
            ).start()

        for_peers(put)

    def wait_sent(phase, c, src):
        part = src.at[c, pl.ds(0, (DEV - 1) * CAP)]
        pltpu.make_async_copy(part, part, send_sem.at[phase, c]).wait()

    def wait_received(phase, c, dst):
        pltpu.make_async_copy(dst.at[c], dst.at[c], recv_sem.at[phase, c]).wait()

    def cols(c):
        return pl.ds(pl.multiple_of(c * W, W), W)

    def tile(i):
        return pl.ds(pl.multiple_of(i * TILE, TILE), TILE)

    live = iota((CAP, DEV), 0) < count_ref[...]
    walks = jnp.where(live, swalk_ref[...], 0)
    table[...] = jnp.zeros_like(table)
    table[:CAP, :] = (walks * 512 + spin_ref[...]).astype(F32)
    packed = table[...].T.astype(jnp.int32)
    pin_hi = ((packed // 256) % 2).astype(F32)
    pin_lo = (packed % 256).astype(F32)
    walk_tab = (packed // 512).astype(F32)
    pin_col = to_column(pin_hi) * 256.0 + to_column(pin_lo)
    pin_t[...] = (iota((SLOTS, PINS), 1).astype(F32) == pin_col).astype(F32).astype(BF)
    loads[0].wait()
    loads[1].wait()

    def project(c):
        value = mm(feat[...], wm[:, cols(c)])
        pre[:, cols(c)] = value
        hid[:, cols(c)] = (value * jax.nn.sigmoid(value)).astype(BF)

        @pl.loop(0, SLOTS // TILE)
        def _(i):
            s0[c, tile(i)] = mm(pin_t[tile(i), :], hid[:, cols(c)]).astype(BF)

    project(0)
    pl.semaphore_wait(barrier, DEV - 1)
    send(0, 0, s0, ra)
    project(1)
    send(0, 1, s0, ra)

    table[:CAP, :] = (walks * 256 + sboard_ref[...]).astype(F32)
    table[...] = table[...].T

    @pl.loop(0, DEV)
    def _(row):
        idx_s[row] = table[pl.ds(row, 1), :].astype(jnp.int32)

    pltpu.make_async_copy(idx_s.at[me], idx_r.at[me], idx_sem.at[1]).start()

    def put_table(peer):
        pltpu.make_async_remote_copy(
            idx_s.at[peer[0] * 4 + peer[1]], idx_r.at[me], idx_sem.at[0], idx_sem.at[1],
            device_id=peer, device_id_type=MESH,
        ).start()

    for_peers(put_table)

    @pl.loop(2, C)
    def _(c):
        project(c)
        send(0, c, s0, ra)

    pltpu.make_async_copy(idx_r, idx_r, idx_sem.at[1]).wait()
    sent_idx = idx_s.at[pl.ds(0, DEV - 1)]
    pltpu.make_async_copy(sent_idx, sent_idx, idx_sem.at[0]).wait()

    @pl.loop(0, DEV)
    def _(row):
        table[pl.ds(row, 1), :] = idx_r[row].astype(F32)

    received = table[...].astype(jnp.int32)
    brd_tab = (received % 256).astype(F32)
    bwalk_tab = (received // 256).astype(F32)
    brd_t[...] = (iota((SLOTS, BOARDS), 1).astype(F32) == to_column(brd_tab)).astype(F32).astype(BF)
    walk_col[...] = to_column(bwalk_tab)
    match = iota((BOARDS, SLOTS), 0).astype(F32) == to_row(brd_tab)
    weights = jnp.where(match, to_row(bwalk_tab), 0.0)
    brd_w[...] = weights.astype(BF)
    bdeg[...] = jnp.maximum(jnp.sum(weights, axis=1, keepdims=True), 1.0)

    @pl.loop(0, C)
    def _(c):
        wait_received(0, c, ra)
        brow_buf[0] = (mm(brd_w[...], ra[c]) / bdeg[...]).astype(BF)

        @pl.loop(0, SLOTS // TILE)
        def _(i):
            s1[c, tile(i)] = mm(brd_t[tile(i), :], brow_buf[0]).astype(BF)

        send(1, c, s1, rb)

    pin_row = to_row(pin_hi) * 256.0 + to_row(pin_lo)
    walk_row = to_row(walk_tab)
    match = iota((PINS, SLOTS), 0).astype(F32) == pin_row
    weights = jnp.where(match, walk_row, 0.0)
    pin_w[...] = weights.astype(BF)
    pdeg[...] = jnp.maximum(jnp.sum(weights, axis=1, keepdims=True), 1.0)
    own_walk = to_column(walk_tab)
    degree_row = jnp.sum(pin_t[...].astype(F32) * own_walk, axis=0, keepdims=True)
    slot_degree = jnp.sum(pin_t[...].astype(F32) * degree_row, axis=1, keepdims=True)
    scale_col[...] = own_walk / jnp.maximum(slot_degree, 1.0)
    feat_t[...] = feat[...].T

    brd_w[...] = (brd_w[...].astype(F32) > 0.0).astype(F32).astype(BF)
    loads[2].wait()
    loads[3].wait()
    upd[...] = jnp.zeros_like(upd)

    @pl.loop(0, C)
    def _(c):
        wait_received(1, c, rb)
        part = (mm(pin_w[...], rb[c]) / pdeg[...]).astype(BF)
        small[...] = part
        nb_t[cols(c), :] = part.T

        @pl.loop(0, C)
        def _(n):
            upd[:, cols(n)] += mm(small[...], wu[cols(c), cols(n)])

    @pl.loop(0, C)
    def _(n):
        feat[:, cols(n)] = (cot[:, cols(n)].astype(F32) * silu_slope(upd[:, cols(n)])).astype(BF)

    @pl.loop(0, C)
    def _(c):
        wait_sent(0, c, s0)
        small[...] = mm(feat[:, :H], wu[cols(c), :], ((1,), (1,))).astype(BF)

        @pl.loop(0, SLOTS // TILE)
        def _(i):
            s0[c, tile(i)] = (scale_col[tile(i), :] * mm(pin_t[tile(i), :], small[...])).astype(BF)

        send(2, c, s0, ra)

    @pl.loop(0, C)
    def _(n):
        wu[cols(n), :] = mm(nb_t[cols(n), :], feat[:, :H]).astype(BF)

    update_steps = [
        grad_steps(wu, gu, 0, i, grad_buf.at[i // 2], (i % 2) * 1024, axis, gsend_sem.at[i], grecv_sem.at[i])
        for i, axis in enumerate((2, 0, 2, 1))
    ]
    for steps in update_steps:
        steps[0]()

    @pl.loop(0, C)
    def _(n):
        update = upd[:, cols(n)]
        out[:, cols(n)] = (hid[:, cols(n)].astype(F32) + update * jax.nn.sigmoid(update)).astype(BF)

    pin_w[...] = (pin_w[...].astype(F32) > 0.0).astype(F32).astype(BF)

    for c in range(C):
        wait_received(2, c, ra)
        wait_sent(1, c, s1)
        board_grad = mm(brd_w[...], ra[c]) / bdeg[...]
        high = board_grad.astype(BF)
        brow_buf[0] = high
        brow_buf[1] = (board_grad - high.astype(F32)).astype(BF)

        @pl.loop(0, SLOTS // TILE)
        def _(i):
            pick = brd_t[tile(i), :]
            rows = mm(pick, brow_buf[0]) + mm(pick, brow_buf[1])
            s1[c, tile(i)] = (walk_col[tile(i), :] * rows).astype(BF)

        send(3, c, s1, rb)

    message_steps = []
    for c in range(C):
        wait_received(3, c, rb)
        grad = cot[:, cols(c)].astype(F32) + mm(pin_w[...], rb[c])
        small[...] = (grad * silu_slope(pre[:, cols(c)])).astype(BF)

        @pl.loop(0, F // TILE)
        def _(i):
            wm[tile(i), cols(c)] = mm(feat_t[tile(i), :], small[...]).astype(BF)

        message_steps.append([
            grad_steps(
                wm, gm, h * 1024, c, ra.at[c], h * 1024, (2 * c + h) % 3,
                gsend_sem.at[4 + 2 * c + h], grecv_sem.at[4 + 2 * c + h],
            )
            for h in range(2)
        ])
        blocks = [update_steps] + message_steps
        for block_set, step in PLAN[c]:
            for steps in blocks[block_set]:
                steps[step]()

    @pl.loop(0, C)
    def _(c):
        wait_sent(2, c, s0)
        wait_sent(3, c, s1)

    for steps in update_steps + message_steps[0] + message_steps[1] + message_steps[2] + message_steps[3]:
        steps[7]()


def store_kernel(a, b, c, x, y, z, sems):
    copies = [pltpu.make_async_copy(s, d, sems.at[i]) for i, (s, d) in enumerate(((a, x), (b, y), (c, z)))]
    for copy in copies:
        copy.start()
    for copy in copies:
        copy.wait()


def finish_results(*results):
    vmem = pl.BlockSpec(memory_space=pltpu.VMEM)
    hbm = pl.BlockSpec(memory_space=pl.ANY)
    return pl.pallas_call(
        store_kernel,
        out_shape=tuple(pltpu.HBM(r.shape, r.dtype) for r in results),
        in_specs=[vmem] * 3,
        out_specs=(hbm,) * 3,
        scratch_shapes=[pltpu.SemaphoreType.DMA((3,))],
        name="store",
        compiler_params=pltpu.CompilerParams(vmem_limit_bytes=8 * 1024 * 1024),
    )(*results)


def body(features, w_message, w_update, cotangent, slot_pin, slot_board, slot_walk, pair_count):
    hbm = pl.BlockSpec(memory_space=pl.ANY)
    vmem = pl.BlockSpec(memory_space=pltpu.VMEM)
    sem = pltpu.SemaphoreType.DMA
    output, gm, gu = pl.pallas_call(
        main_kernel,
        out_shape=(
            pltpu.VMEM((PINS, H), BF),
            pltpu.VMEM((F, H), BF),
            pltpu.VMEM((H, H), BF),
        ),
        in_specs=[hbm] * 4 + [vmem] * 4,
        out_specs=(vmem, vmem, vmem),
        scratch_shapes=[
            pltpu.VMEM((PINS, F), BF), pltpu.VMEM((F, H), BF), pltpu.VMEM((H, H), BF), pltpu.VMEM((PINS, H), BF),
            pltpu.VMEM((PINS, H), F32), pltpu.VMEM((PINS, H), BF),
            pltpu.VMEM((C, SLOTS, W), BF), pltpu.VMEM((C, SLOTS, W), BF),
            pltpu.VMEM((C, SLOTS, W), BF), pltpu.VMEM((C, SLOTS, W), BF),
            pltpu.VMEM((SLOTS, PINS), BF), pltpu.VMEM((PINS, SLOTS), BF),
            pltpu.VMEM((SLOTS, BOARDS), BF), pltpu.VMEM((BOARDS, SLOTS), BF),
            pltpu.VMEM((F, PINS), BF),
            pltpu.VMEM((PINS, H), F32), pltpu.VMEM((H, PINS), BF),
            pltpu.VMEM((SLOTS, 1), F32), pltpu.VMEM((SLOTS, 1), F32), pltpu.VMEM((PINS, 1), F32), pltpu.VMEM((BOARDS, 1), F32),
            pltpu.VMEM((2, BOARDS, W), BF), pltpu.VMEM((2, SLOTS, W), BF), pltpu.VMEM((PINS, W), BF),
            pltpu.VMEM((DEV, DEV), F32), pltpu.VMEM((DEV, 1, DEV), jnp.int32), pltpu.VMEM((DEV, 1, DEV), jnp.int32),
            sem((4,)), sem((2,)), sem((4, C)), sem((4, C)), sem((12, 6)), sem((12, 6)),
        ],
        name="layer",
        compiler_params=pltpu.CompilerParams(
            collective_id=0, has_side_effects=True, vmem_limit_bytes=54 * 1024 * 1024
        ),
    )(
        features, w_message, w_update, cotangent,
        slot_pin[0].T, slot_board[0].T, slot_walk[0].T, pair_count,
    )
    return finish_results(output, gm, gu)


def solution(mesh):
    in_specs = (
        P(("pin", "board"), None),
        P(),
        P(),
        P(("pin", "board"), None),
        P(("pin", "board"), None, None),
        P(("pin", "board"), None, None),
        P(("pin", "board"), None, None),
        P(("pin", "board"), None),
    )
    out_specs = (P(("pin", "board"), None), P(), P())
    return jax.shard_map(body, mesh=mesh, in_specs=in_specs, out_specs=out_specs, check_vma=False)
```
